32 devices in a mesh: groups: 2 (over y), hist: 2 (over x), rows: 4 (over z), cols: 2 (over core).
Axes of the slice: x: 2, y: 2, z: 4, core: 2. Of those that a mesh axis runs over, the one named last changes fastest.
Arguments:
- hists: float32 [2, 1024, 4096], P('hist', ('groups', 'rows'), 'cols'), parts along dimension 1, may hold values from 0.2 to 2000, as said below
- log_scaling_fields: float32 [2, 1024, 4096], P('hist', ('groups', 'rows'), 'cols'), parts along dimension 1, may hold values from -1 to 1
- histogram_weight_list: float32 [2], replicated, may hold values from 0.25 to 4
Outputs:
- barycenter: float32 [1024, 4096], P(('groups', 'rows'), 'cols'), parts along dimension 0
- new_logs: float32 [2, 1024, 4096], P('hist', ('groups', 'rows'), 'cols'), parts along dimension 1
The draws below stay inside these ranges and needn't reach their ends.
There are 2 independent parts, one for each index of `groups`. The reference program is written for one: setup_inputs(seed, part) draws one part's arguments, and reference() takes and returns one part's arrays. A program takes and returns all parts, laid end to end along the dimension named above; an argument that names none is the same for every part. Nothing has to cross between parts.
Inputs may be any that keep to these rules, and one draw needn't show every extreme that they name: `hists`: every entry is positive.
All inputs are finite; a program needn't handle non-finite values.
Results may differ from the reference program's by a relative error of at most 0.00021.
Values sent between devices are 32-bit elements; how exact they have to be, the bound alone decides.
No kernel may reach another device: no remote copies, remote signals or barrier semaphores. Data moves between devices by JAX's collectives and lax.ppermute only.
A program may use at most 64 MiB of HBM per device.

```python
import math
import jax
import jax.numpy as jnp
from jax import lax

HALF = 32
NHIST = 2
HEIGHT = 512
WIDTH = 4096


def draw_hists(key, part):
    row_key = jax.random.fold_in(key, 11)
    col_key = jax.random.fold_in(key, 12)
    cell_key = jax.random.fold_in(key, 13)
    row_index = jnp.arange(HEIGHT).astype(jnp.float32) / float(max(HEIGHT - 1, 1))
    row_random = jnp.exp(jax.random.uniform(row_key, (HEIGHT,), jnp.float32) * math.log(4.0))
    row_trend = jnp.exp(row_index * math.log(3.0))
    col_scale = jnp.exp(jax.random.uniform(col_key, (WIDTH,), jnp.float32) * math.log(10.0))
    rough_cells = jnp.exp(jax.random.uniform(cell_key, (NHIST, HEIGHT, WIDTH), jnp.float32, -1.0, 1.0))
    row_scale = row_trend * row_random
    return (rough_cells * row_scale[None, :, None] * col_scale[None, None, :]).astype(jnp.float32)


def draw_log_scaling_fields(key, part):
    term_total = 8
    wave_key = jax.random.fold_in(key, 21)
    angle_key = jax.random.fold_in(key, 22)
    phase_key = jax.random.fold_in(key, 23)
    rough_key = jax.random.fold_in(key, 24)
    wave_lengths = 32.0 * jnp.exp(jax.random.uniform(wave_key, (NHIST, term_total), jnp.float32) * math.log(16.0))
    angle_draws = jax.random.uniform(angle_key, (NHIST, term_total), jnp.float32, 0.0, 2.0 * math.pi)
    phase_draws = jax.random.uniform(phase_key, (NHIST, term_total), jnp.float32, 0.0, 2.0 * math.pi)
    row_at = jnp.arange(HEIGHT).astype(jnp.float32)[None, :, None]
    col_at = jnp.arange(WIDTH).astype(jnp.float32)[None, None, :]
    smooth_sum = jnp.zeros((NHIST, HEIGHT, WIDTH), jnp.float32)
    for term_index in range(term_total):
        freq_here = 2.0 * math.pi / wave_lengths[:, term_index]
        freq_rows = (freq_here * jnp.cos(angle_draws[:, term_index]))[:, None, None]
        freq_cols = (freq_here * jnp.sin(angle_draws[:, term_index]))[:, None, None]
        smooth_sum = smooth_sum + jnp.cos(freq_rows * row_at + freq_cols * col_at + phase_draws[:, term_index][:, None, None])
    rough_part = jax.random.uniform(rough_key, (NHIST, HEIGHT, WIDTH), jnp.float32, -1.0, 1.0)
    inner = 0.45 * smooth_sum + 0.15 * rough_part
    return (0.98 * jnp.tanh(inner)).astype(jnp.float32)


def setup_inputs(seed: int = 0, part: int = 0) -> dict:
    key_list = jax.random.split(jax.random.key(seed), 4)
    part_splits = jax.random.split(jax.random.fold_in(key_list[3], part), 4)
    hists = draw_hists(jax.random.fold_in(jax.random.fold_in(key_list[3], part), 71), part)
    log_scaling_fields = draw_log_scaling_fields(jax.random.fold_in(jax.random.fold_in(key_list[3], part), 71), part)
    histogram_weight_list = jnp.clip(jnp.exp(jax.random.uniform(key_list[2], (NHIST,), jnp.float32, math.log(0.25), math.log(4.0))), 0.25, 4.0)
    return dict(hists=hists, log_scaling_fields=log_scaling_fields, histogram_weight_list=histogram_weight_list)


kernel_sigma = 16.0


def kernel_profile():
    offsets = jnp.arange(-HALF, HALF + 1).astype(jnp.float32)
    raw_taps = jnp.exp(-offsets * offsets / (2.0 * kernel_sigma * kernel_sigma))
    return raw_taps / jnp.sum(raw_taps)


def blurred_field(fields):
    stacked = fields[:, None]
    profile = kernel_profile()
    across = lax.conv_general_dilated(stacked, profile.reshape(1, 1, 1, -1), (1, 1), ((0, 0), (HALF, HALF)), precision=lax.Precision.HIGHEST)
    vertical = lax.conv_general_dilated(across, profile.reshape(1, 1, -1, 1), (1, 1), ((HALF, HALF), (0, 0)), precision=lax.Precision.HIGHEST)
    return vertical[:, 0]


def reference(hists, log_scaling_fields, histogram_weight_list):
    scaling_fields = jnp.exp(log_scaling_fields)
    blurred_vertical = blurred_field(scaling_fields)
    ratios = hists / blurred_vertical
    smooth_u = blurred_field(ratios)
    log_blurred = jnp.log(smooth_u)
    log_portions = log_scaling_fields + log_blurred
    lambdas = histogram_weight_list / jnp.sum(histogram_weight_list)
    log_mean = jnp.sum(lambdas[:, None, None] * log_portions, axis=0)
    mean_field = jnp.exp(log_mean)
    total_mass = jnp.sum(mean_field)
    barycenter = mean_field * (HEIGHT * WIDTH / total_mass)
    new_logs = jnp.log(barycenter)[None] - log_blurred
    return (barycenter, new_logs)
```

```python
import functools

import jax
import jax.numpy as jnp
import numpy as np
from jax import lax
from jax.experimental import pallas as pl
from jax.experimental.pallas import tpu as pltpu
from jax.sharding import PartitionSpec as P

HALF = 32
LANES = 128
kernel_sigma = 16.0


def band_matrix(rows_in, cols_out):
    taps = np.arange(-HALF, HALF + 1).astype(np.float64)
    total = np.sum(np.exp(-taps * taps / (2.0 * kernel_sigma * kernel_sigma)))
    offsets = np.arange(rows_in)[:, None] - np.arange(cols_out)[None, :] - HALF
    entries = np.exp(-offsets * offsets / (2.0 * kernel_sigma * kernel_sigma)) / total
    return np.where(np.abs(offsets) <= HALF, entries, 0.0).astype(np.float32)


def split_constant(matrix):
    high = matrix.astype(jnp.bfloat16)
    low = (matrix - high.astype(np.float32)).astype(jnp.bfloat16)
    return high, low


def column_band():
    high, low = split_constant(band_matrix(LANES + 2 * HALF, LANES))
    return jnp.asarray(np.concatenate([high, low], axis=1))


def row_band(rows_out):
    high, low = split_constant(band_matrix(rows_out + 2 * HALF, rows_out).T)
    return jnp.asarray(
        np.concatenate(
            [np.concatenate([high, high], axis=1), np.concatenate([low, np.zeros_like(low)], axis=1)], axis=0
        )
    )


def split(values):
    high = values.astype(jnp.bfloat16)
    low = (values - high.astype(jnp.float32)).astype(jnp.bfloat16)
    return high, low


def dot(left, right):
    return jnp.dot(left, right, preferred_element_type=jnp.float32)


def column_block(window, band):
    high, low = split(window)
    depth = window.shape[1]
    both = dot(high, band[:depth])
    return both[:, :LANES] + both[:, LANES:] + dot(low, band[:depth, :LANES])


def row_block(window, band):
    high, low = split(window)
    rows = band.shape[0] // 2
    both = dot(band, jnp.concatenate([high, low], axis=0))
    return both[:rows] + both[rows:]


def edge_flags():
    place = lax.axis_index("cols")
    return (place > 0).astype(jnp.float32), (place < lax.axis_size("cols") - 1).astype(jnp.float32)


def spread_kernel(logs, from_left, from_right, band, across, top, bottom, wide):
    has_left, has_right = edge_flags()
    width = logs.shape[1]
    edge = 2 * HALF
    wide[:, :] = jnp.concatenate(
        [from_left[:, :edge] * has_left, jnp.exp(logs[...]), from_right[:, :edge] * has_right], axis=1
    )
    taps = band[...]
    for start in range(0, width + edge, LANES):
        stop = min(start + LANES + 2 * HALF, width + 2 * edge)
        across[:, start : start + LANES] = column_block(wide[:, start:stop], taps)
    top[...] = across[:HALF, :]
    bottom[...] = across[across.shape[0] - HALF :, :]


def ratio_rows(smooth, masses, from_left, from_right):
    has_left, has_right = edge_flags()
    edge = 2 * HALF
    rows = masses.shape[0]
    wide = jnp.concatenate(
        [
            from_left[:, edge : edge + HALF] * has_left,
            masses,
            from_right[:, edge : edge + HALF] * has_right,
            jnp.zeros((rows, edge), jnp.float32),
        ],
        axis=1,
    )
    return jnp.where(wide > 0.0, wide / smooth, 0.0)


def chunks(width, step):
    return [(start, min(start + step, width)) for start in range(0, width, step)]


def column_pass(ratios, taps, out):
    for start in range(0, out.shape[1], LANES):
        out[:, start : start + LANES] = column_block(ratios[:, start : start + LANES + 2 * HALF], taps)


def inner_ratio_kernel(across, masses, from_left, from_right, band, rows_band, out, smooth, ratios):
    height = masses.shape[0]
    for start, stop in chunks(across.shape[1], 256):
        smooth[:, start:stop] = row_block(across[:, start:stop], rows_band[...])
    inner = slice(HALF, height - HALF)
    ratios[...] = ratio_rows(smooth[...], masses[inner, :], from_left[inner, :], from_right[inner, :])
    column_pass(ratios, band[...], out)


def rim_ratio_kernel(
    across, above, below, masses, from_left, from_right, band, rows_band, top, bottom, smooth, ratios, out
):
    height = masses.shape[0]
    taps = rows_band[...]
    for start, stop in chunks(across.shape[1], 256):
        upper = jnp.concatenate([above[:, start:stop], across[: 2 * HALF, start:stop]], axis=0)
        lower = jnp.concatenate([across[height - 2 * HALF :, start:stop], below[:, start:stop]], axis=0)
        smooth[:HALF, start:stop] = row_block(upper, taps)
        smooth[HALF:, start:stop] = row_block(lower, taps)
    rims = lambda ref: jnp.concatenate([ref[:HALF, :], ref[height - HALF :, :]], axis=0)
    ratios[...] = ratio_rows(smooth[...], rims(masses), rims(from_left), rims(from_right))
    column_pass(ratios, band[...], out)
    top[...] = out[:HALF, :]
    bottom[...] = out[HALF:, :]


def write_parts(weight, log_rows, log_smooth, own, first, later):
    own[...] = weight * (log_rows + log_smooth)
    count = lax.axis_size("hist")
    place = lax.axis_index("hist")
    share = own.shape[1] // count
    for shift in range(1, count):
        other = lax.rem(place + shift, count)
        first[shift - 1] = own[:, pl.ds(pl.multiple_of(other * share, LANES), share)]
        for step in range(1, count):
            block = lax.rem(other + step, count)
            later[shift - 1, :, (step - 1) * share : step * share] = own[
                :, pl.ds(pl.multiple_of(block * share, LANES), share)
            ]


def inner_log_kernel(weight, top, inner, bottom, logs, rows_band, smooth, own, first, later):
    height = logs.shape[0]
    taps = rows_band[...]
    for start, stop in chunks(inner.shape[1], 256):
        window = jnp.concatenate([top[:, start:stop], inner[:, start:stop], bottom[:, start:stop]], axis=0)
        smooth[:, start:stop] = jnp.log(row_block(window, taps))
    write_parts(weight[0, 0], logs[HALF : height - HALF, :], smooth[...], own, first, later)


def rim_log_kernel(weight, above, top, inner, bottom, below, logs, rows_band, smooth, own, first, later):
    height = logs.shape[0]
    depth = inner.shape[0]
    taps = rows_band[...]
    for start, stop in chunks(inner.shape[1], 256):
        part = lambda ref, rows=slice(None): ref[rows, start:stop]
        upper = jnp.concatenate([part(above), part(top), part(inner, slice(0, HALF))], axis=0)
        lower = jnp.concatenate([part(inner, slice(depth - HALF, depth)), part(bottom), part(below)], axis=0)
        smooth[:HALF, start:stop] = jnp.log(row_block(upper, taps))
        smooth[HALF:, start:stop] = jnp.log(row_block(lower, taps))
    log_rows = jnp.concatenate([logs[:HALF, :], logs[height - HALF :, :]], axis=0)
    write_parts(weight[0, 0], log_rows, smooth[...], own, first, later)


def whole(count):
    return [pl.BlockSpec(memory_space=pltpu.VMEM)] * count


def call(kernel, name, args, outs, scratch=(), scalars=0, cost=0):
    f32 = lambda shape: jax.ShapeDtypeStruct(shape, jnp.float32)
    return pl.pallas_call(
        kernel,
        name=name,
        out_shape=tuple(f32(shape) for shape in outs),
        in_specs=[pl.BlockSpec(memory_space=pltpu.SMEM)] * scalars + whole(len(args) - scalars),
        out_specs=tuple(whole(len(outs))),
        scratch_shapes=[pltpu.VMEM(shape, jnp.float32) for shape in scratch],
        compiler_params=pltpu.CompilerParams(vmem_limit_bytes=32 * 1024 * 1024),
        cost_estimate=pl.CostEstimate(flops=cost, bytes_accessed=cost // 256, transcendentals=0),
    )(*args)


def swap_columns(right_edge, left_edge):
    count = lax.axis_size("cols")
    if count == 2:
        sent = jnp.where(lax.axis_index("cols") == 0, right_edge, left_edge)
        got = lax.ppermute(sent, "cols", [(0, 1), (1, 0)])
        return got, got
    steps = [(i, i + 1) for i in range(count - 1)]
    return (
        lax.ppermute(right_edge, "cols", steps),
        lax.ppermute(left_edge, "cols", [(b, a) for a, b in steps]),
    )


def swap_rows(top, bottom):
    steps = [(i, i + 1) for i in range(lax.axis_size("rows") - 1)]
    return lax.ppermute(bottom, "rows", steps), lax.ppermute(top, "rows", [(b, a) for a, b in steps])


def share_over_hist(parts):
    count = lax.axis_size("hist")
    return [
        lax.ppermute(parts[shift - 1], "hist", [(i, (i + shift) % count) for i in range(count)])
        for shift in range(1, count)
    ]


def total_over(values, axes):
    for axis in axes:
        count = lax.axis_size(axis)
        span = 1
        while span < count:
            values = values + lax.ppermute(values, axis, [(i, i ^ span) for i in range(count)])
            span *= 2
    return values


def gathered_mean(own, first, later):
    count = lax.axis_size("hist")
    place = lax.axis_index("hist")
    share = own.shape[1] // count
    mine = lax.dynamic_slice_in_dim(own, place * share, share, axis=1) + sum(first)
    return mine, later


def body(hists, log_scaling_fields, histogram_weight_list):
    masses = hists[0]
    logs = log_scaling_fields[0]
    height, width = masses.shape
    count = lax.axis_size("hist")
    place = lax.axis_index("hist")
    edge = 2 * HALF
    inner = height - edge
    taps = column_band()
    inner_taps = row_band(inner)
    rim_taps = row_band(HALF)

    own_pick = lax.broadcasted_iota(jnp.int32, histogram_weight_list.shape, 0) == place
    weight = jnp.sum(jnp.where(own_pick, histogram_weight_list, 0.0)) / jnp.sum(histogram_weight_list)
    weight = weight.reshape(1, 1)

    gap = jnp.zeros((height, LANES - edge - HALF), jnp.float32)
    right_edge = jnp.concatenate([jnp.exp(logs[:, width - edge :]), masses[:, width - HALF :], gap], axis=1)
    left_edge = jnp.concatenate([jnp.exp(logs[:, :edge]), masses[:, :HALF], gap], axis=1)
    from_left, from_right = swap_columns(right_edge, left_edge)

    wide = width + LANES
    matmul = 2 * height * width * 3 * 256
    across, top, bottom = call(
        spread_kernel, "spread", (logs, from_left, from_right, taps),
        [(height, wide), (HALF, wide), (HALF, wide)], [(height, wide)], cost=matmul,
    )
    above, below = swap_rows(top, bottom)
    (second,) = call(
        inner_ratio_kernel, "inner_ratio", (across, masses, from_left, from_right, taps, inner_taps),
        [(inner, width)], [(inner, wide), (inner, wide)], cost=matmul,
    )
    second_top, second_bottom = call(
        rim_ratio_kernel, "rim_ratio", (across, above, below, masses, from_left, from_right, taps, rim_taps),
        [(HALF, width), (HALF, width)], [(edge, wide), (edge, wide), (edge, width)], cost=matmul,
    )
    second_above, second_below = swap_rows(second_top, second_bottom)

    share = width // count
    parts = [
        ((inner, width), (inner, width), (count - 1, inner, share), (count - 1, inner, width - share)),
        ((edge, width), (edge, width), (count - 1, edge, share), (count - 1, edge, width - share)),
    ]
    in_smooth, in_own, in_first, in_later = call(
        inner_log_kernel, "inner_log", (weight, second_top, second, second_bottom, logs, inner_taps),
        parts[0], scalars=1, cost=matmul,
    )
    in_first = share_over_hist(in_first)
    rim_smooth, rim_own, rim_first, rim_later = call(
        rim_log_kernel, "rim_log",
        (weight, second_above, second_top, second, second_bottom, second_below, logs, rim_taps),
        parts[1], scalars=1, cost=matmul,
    )
    rim_first = share_over_hist(rim_first)
    in_later = share_over_hist(in_later)
    rim_later = share_over_hist(rim_later)

    def own_share(own, first):
        return lax.dynamic_slice_in_dim(own, place * share, share, axis=1) + sum(first)

    partial = jnp.sum(jnp.exp(own_share(in_own, in_first)).reshape(-1, 8, share), axis=0) + jnp.sum(
        jnp.exp(own_share(rim_own, rim_first)).reshape(-1, 8, share), axis=0
    )
    partial = jnp.sum(partial.reshape(8, -1, LANES), axis=1)
    total = jnp.sum(total_over(partial, ("cols", "rows", "hist")))
    scale = height * lax.axis_size("rows") * width * lax.axis_size("cols") / total

    def log_mean(own, first, later):
        others = jnp.zeros_like(own)
        mine = lax.broadcasted_iota(jnp.int32, own.shape, 1) // share == place
        if count == 2:
            arrived = jnp.where(
                mine,
                jnp.concatenate([first[0], first[0]], axis=1),
                jnp.concatenate([later[0], later[0]], axis=1),
            )
            return own + arrived
        others = lax.dynamic_update_slice_in_dim(others, sum(first), place * share, axis=1)
        for shift in range(1, count):
            for step in range(1, count):
                block = lax.rem(place + step, count)
                piece = later[shift - 1][:, (step - 1) * share : step * share]
                start = block * share
                now = lax.dynamic_slice_in_dim(others, start, share, axis=1)
                others = lax.dynamic_update_slice_in_dim(others, now + piece, start, axis=1)
        return own + others

    def joined(inner_rows, rim_rows):
        return jnp.concatenate([rim_rows[:HALF], inner_rows, rim_rows[HALF:]], axis=0)

    mean = joined(log_mean(in_own, in_first, in_later), log_mean(rim_own, rim_first, rim_later))
    log_smooth = joined(in_smooth, rim_smooth)
    barycenter = jnp.exp(mean) * scale
    new_logs = mean + jnp.log(scale) - log_smooth
    return (barycenter, new_logs[None])


def solution(mesh):
    return jax.shard_map(
        body,
        mesh=mesh,
        in_specs=(
            P("hist", ("groups", "rows"), "cols"),
            P("hist", ("groups", "rows"), "cols"),
            P(),
        ),
        out_specs=(P(("groups", "rows"), "cols"), P("hist", ("groups", "rows"), "cols")),
        check_vma=False,
    )
```

```python
import functools

import jax
import jax.numpy as jnp
import numpy as np
from jax import lax
from jax.experimental import pallas as pl
from jax.experimental.pallas import tpu as pltpu
from jax.sharding import PartitionSpec as P

HALF = 32
LANES = 128
kernel_sigma = 16.0


def taps_total():
    taps = np.arange(-HALF, HALF + 1).astype(np.float64)
    return float(np.sum(np.exp(-taps * taps / (2.0 * kernel_sigma * kernel_sigma))))


def band_matrix(shape, axis_in):
    places = lax.broadcasted_iota(jnp.int32, shape, axis_in) - lax.broadcasted_iota(jnp.int32, shape, 1 - axis_in)
    offsets = (places - HALF).astype(jnp.float32)
    entries = jnp.exp(-offsets * offsets / (2.0 * kernel_sigma * kernel_sigma)) / taps_total()
    return jnp.where(jnp.abs(offsets) <= HALF, entries, 0.0)


def column_band():
    high, low = split(band_matrix((LANES + 2 * HALF, LANES), 0))
    return jnp.concatenate([high, low], axis=1)


def row_band(rows_out):
    high, low = split(band_matrix((rows_out, rows_out + 2 * HALF), 1))
    return jnp.concatenate(
        [jnp.concatenate([high, high], axis=1), jnp.concatenate([low, jnp.zeros_like(low)], axis=1)], axis=0
    )


def split(values):
    high = values.astype(jnp.bfloat16)
    low = (values - high.astype(jnp.float32)).astype(jnp.bfloat16)
    return high, low


def dot(left, right):
    return jnp.dot(left, right, preferred_element_type=jnp.float32)


def column_block(window, band):
    high, low = split(window)
    depth = window.shape[1]
    both = dot(high, band[:depth])
    return both[:, :LANES] + both[:, LANES:] + dot(low, band[:depth, :LANES])


def row_block(window, band):
    high, low = split(window)
    rows = band.shape[0] // 2
    both = dot(band, jnp.concatenate([high, low], axis=0))
    return both[:rows] + both[rows:]


def edge_flags():
    place = lax.axis_index("cols")
    return (place > 0).astype(jnp.float32), (place < lax.axis_size("cols") - 1).astype(jnp.float32)


def row_parity():
    return lax.rem(lax.axis_index("rows"), 2)


def chunks(width, step):
    return [(start, min(start + step, width)) for start in range(0, width, step)]


def edge_sides():
    return [lax.axis_index("cols") == 0] if lax.axis_size("cols") == 2 else [True, False]


def edge_kernel(function, values, *refs):
    outs = refs[-len(edge_sides()) :]
    width = values.shape[1]
    for out, right in zip(outs, edge_sides()):
        start = pl.multiple_of(jnp.where(right, width - LANES, 0), LANES)
        out[...] = function(values[:, pl.ds(start, LANES)])


def spread_kernel(logs, across, wide):
    width = logs.shape[1]
    edge = 2 * HALF
    taps = column_band()
    wide[:, edge : edge + width] = jnp.exp(logs[...])
    for start in range(LANES, width, LANES):
        across[:, start : start + LANES] = column_block(wide[:, start : start + LANES + 2 * HALF], taps)


def spread_edge_kernel(partial, logs, from_left, from_right, across, first, second):
    has_left, has_right = edge_flags()
    height, width = logs.shape
    edge = 2 * HALF
    taps = column_band()
    across[...] = partial[...]
    left = jnp.concatenate([from_left[:, edge:] * has_left, jnp.exp(logs[:, :LANES])], axis=1)
    right = jnp.concatenate([jnp.exp(logs[:, width - edge :]), from_right[:, :edge] * has_right], axis=1)
    across[:, :LANES] = column_block(left, taps)
    across[:, width : width + LANES] = column_block(right, taps)
    odd = row_parity()
    first[...] = across[pl.ds(pl.multiple_of((1 - odd) * (height - HALF), HALF), HALF), :]
    second[...] = across[pl.ds(pl.multiple_of(odd * (height - HALF), HALF), HALF), :]


def ratio_rows(smooth, masses, from_left, from_right):
    has_left, has_right = edge_flags()
    edge = 2 * HALF
    rows = masses.shape[0]
    wide = jnp.concatenate(
        [
            from_left[:, LANES - HALF :] * has_left,
            masses,
            from_right[:, :HALF] * has_right,
            jnp.zeros((rows, edge), jnp.float32),
        ],
        axis=1,
    )
    return jnp.where(wide > 0.0, wide / smooth, 0.0)


def column_pass(ratios, taps, out):
    for start in range(0, out.shape[1], LANES):
        out[:, start : start + LANES] = column_block(ratios[:, start : start + LANES + 2 * HALF], taps)


def inner_ratio_kernel(across, masses, from_left, from_right, out, smooth, ratios):
    height = masses.shape[0]
    taps = row_band(out.shape[0])
    for start, stop in chunks(across.shape[1], 256):
        smooth[:, start:stop] = row_block(across[:, start:stop], taps)
    inner = slice(HALF, height - HALF)
    ratios[...] = ratio_rows(smooth[...], masses[inner, :], from_left[inner, :], from_right[inner, :])
    column_pass(ratios, column_band(), out)


def rim_ratio_kernel(
    after, across, first, second, masses, from_left, from_right, rims, sent_first, sent_second,
    smooth, ratios,
):
    height = masses.shape[0]
    taps = row_band(HALF)
    odd = row_parity()
    for start, stop in chunks(across.shape[1], 256):
        one, two = first[:, start:stop], second[:, start:stop]
        upper = jnp.concatenate([jnp.where(odd == 1, one, two), across[: 2 * HALF, start:stop]], axis=0)
        lower = jnp.concatenate(
            [across[height - 2 * HALF :, start:stop], jnp.where(odd == 1, two, one)], axis=0
        )
        smooth[:HALF, start:stop] = row_block(upper, taps)
        smooth[HALF:, start:stop] = row_block(lower, taps)
    ends = lambda ref: jnp.concatenate([ref[:HALF, :], ref[height - HALF :, :]], axis=0)
    ratios[...] = ratio_rows(smooth[...], ends(masses), ends(from_left), ends(from_right))
    column_pass(ratios, column_band(), rims)
    sent_first[...] = rims[pl.ds(pl.multiple_of((1 - odd) * HALF, HALF), HALF), :]
    sent_second[...] = rims[pl.ds(pl.multiple_of(odd * HALF, HALF), HALF), :]


def own_weight(weights):
    total = weights[0]
    for k in range(1, weights.shape[0]):
        total += weights[k]
    return jnp.full((1, 1), weights[lax.axis_index("hist")]) / jnp.full((1, 1), total)


def block_of(ref, place, share):
    return ref[:, pl.ds(pl.multiple_of(place * share, LANES), share)]


def others_first(own, first):
    count = lax.axis_size("hist")
    share = own.shape[1] // count
    for shift in range(1, count):
        other = lax.rem(lax.axis_index("hist") + shift, count)
        first[shift - 1] = block_of(own, other, share)


def inner_log_kernel(weights, rims, inner, logs, smooth, own, first):
    height = logs.shape[0]
    taps = row_band(inner.shape[0])
    for start, stop in chunks(inner.shape[1], 256):
        window = jnp.concatenate([rims[:HALF, start:stop], inner[:, start:stop], rims[HALF:, start:stop]], axis=0)
        smooth[:, start:stop] = jnp.log(row_block(window, taps))
    own[...] = own_weight(weights) * (logs[HALF : height - HALF, :] + smooth[...])
    others_first(own, first)


def rim_log_kernel(
    weights, from_first, from_second, rims, inner, logs, smooth, own, first
):
    height = logs.shape[0]
    depth = inner.shape[0]
    taps = row_band(HALF)
    odd = row_parity()
    for start, stop in chunks(inner.shape[1], 256):
        one, two = from_first[:, start:stop], from_second[:, start:stop]
        above, below = jnp.where(odd == 1, one, two), jnp.where(odd == 1, two, one)
        upper = jnp.concatenate([above, rims[:HALF, start:stop], inner[:HALF, start:stop]], axis=0)
        lower = jnp.concatenate([inner[depth - HALF :, start:stop], rims[HALF:, start:stop], below], axis=0)
        smooth[:HALF, start:stop] = jnp.log(row_block(upper, taps))
        smooth[HALF:, start:stop] = jnp.log(row_block(lower, taps))
    log_rows = jnp.concatenate([logs[:HALF, :], logs[height - HALF :, :]], axis=0)
    own[...] = own_weight(weights) * (log_rows + smooth[...])
    others_first(own, first)


def others_later(inner_own, rim_own, later):
    height = later.shape[1]
    count = lax.axis_size("hist")
    share = rim_own.shape[1] // count
    for shift in range(1, count):
        other = lax.rem(lax.axis_index("hist") + shift, count)
        for step in range(1, count):
            block = lax.rem(other + step, count)
            slot = slice((step - 1) * share, step * share)
            rim = block_of(rim_own, block, share)
            later[shift - 1, :HALF, slot] = rim[:HALF]
            later[shift - 1, HALF : height - HALF, slot] = block_of(inner_own, block, share)
            later[shift - 1, height - HALF :, slot] = rim[HALF:]


def folded(values):
    rows, width = values.shape
    total = jnp.sum(values.reshape(rows // 8, 8, width), axis=0)
    return sum(total[:, start : start + LANES] for start in range(0, width, LANES))


def mean_part(own, smooth, arrived, mean, change):
    share = mean.shape[1]
    place = lax.axis_index("hist")
    log_mean = block_of(own, place, share) + sum(ref[...] for ref in arrived)
    values = jnp.exp(log_mean)
    mean[...] = values
    change[...] = log_mean - block_of(smooth, place, share)
    return folded(values)


def inner_mean_kernel(own, smooth, rim_own, *refs):
    arrived, (mean, change, partial, later) = refs[:-4], refs[-4:]
    others_later(own, rim_own, later)
    partial[...] = mean_part(own, smooth, arrived, mean, change)


def rim_mean_kernel(own, smooth, before, *refs):
    arrived, (mean, change, partial) = refs[:-3], refs[-3:]
    partial[...] = before[...] + mean_part(own, smooth, arrived, mean, change)


def later_mean_kernel(rim_own, rim_smooth, inner_own, inner_smooth, *refs):
    arrived, (mean, change) = refs[:-2], refs[-2:]
    count = lax.axis_size("hist")
    height = mean.shape[0]
    share = rim_own.shape[1] // count
    for step in range(1, count):
        block = lax.rem(lax.axis_index("hist") + step, count)
        slot = slice((step - 1) * share, step * share)
        for rows, own, smooth, part in (
            (slice(0, HALF), rim_own, rim_smooth, slice(0, HALF)),
            (slice(HALF, height - HALF), inner_own, inner_smooth, slice(None)),
            (slice(height - HALF, height), rim_own, rim_smooth, slice(HALF, 2 * HALF)),
        ):
            lanes = pl.ds(pl.multiple_of(block * share, LANES), share)
            log_mean = own[part, lanes] + sum(ref[rows, slot] for ref in arrived)
            mean[rows, slot] = jnp.exp(log_mean)
            change[rows, slot] = log_mean - smooth[part, lanes]


def final_kernel(
    cells, total, rim_mean, rim_change, inner_mean, inner_change, later_mean, later_change, barycenter, new_logs,
    stage, sems,
):
    count = lax.axis_size("hist")
    height, width = barycenter.shape
    share = width // count
    scale = cells / jnp.sum(total[...], axis=(0, 1), keepdims=True)
    log_scale = jnp.log(scale)
    copies = []
    for k, (out, rim, inner, later, apply) in enumerate(
        (
            (barycenter, rim_mean, inner_mean, later_mean, lambda x: x * scale),
            (new_logs, rim_change, inner_change, later_change, lambda x: x + log_scale),
        )
    ):
        for step in range(count):
            slot = slice(step * share, (step + 1) * share)
            if step == 0:
                stage[k, :HALF, slot] = apply(rim[:HALF, :])
                stage[k, HALF : height - HALF, slot] = apply(inner[...])
                stage[k, height - HALF :, slot] = apply(rim[HALF:, :])
            else:
                stage[k, :, slot] = apply(later[:, (step - 1) * share : step * share])
            block = lax.rem(lax.axis_index("hist") + step, count)
            lanes = pl.ds(pl.multiple_of(block * share, LANES), share)
            copy = pltpu.make_async_copy(stage.at[k, :, slot], out.at[:, lanes], sems.at[k, step])
            copy.start()
            copies.append(copy)
    for copy in copies:
        copy.wait()


def call(kernel, name, args, outs, scratch=(), scalars=0, cost=0, far_in=(), far_out=False, sems=None,
         room=32):
    f32 = lambda shape: jax.ShapeDtypeStruct(shape, jnp.float32)
    near = pl.BlockSpec(memory_space=pltpu.VMEM)
    far = pl.BlockSpec(memory_space=pltpu.HBM)
    scalar = pl.BlockSpec(memory_space=pltpu.SMEM)
    return pl.pallas_call(
        kernel,
        name=name,
        out_shape=tuple(f32(shape) for shape in outs),
        in_specs=[scalar if k < scalars else far if k in far_in else near for k in range(len(args))],
        out_specs=tuple(far if far_out else near for _ in outs),
        scratch_shapes=[pltpu.VMEM(shape, jnp.float32) for shape in scratch]
        + ([pltpu.SemaphoreType.DMA(sems)] if sems else []),
        compiler_params=pltpu.CompilerParams(vmem_limit_bytes=room * 1024 * 1024),
        cost_estimate=pl.CostEstimate(flops=5 * cost, bytes_accessed=cost // 256, transcendentals=0),
    )(*args)


def swap_columns(edges):
    count = lax.axis_size("cols")
    if count == 2:
        got = lax.ppermute(edges[0], "cols", [(0, 1), (1, 0)])
        return got, got
    steps = [(i, i + 1) for i in range(count - 1)]
    right_edge, left_edge = edges
    return (
        lax.ppermute(right_edge, "cols", steps),
        lax.ppermute(left_edge, "cols", [(b, a) for a, b in steps]),
    )


def swap_rows(first, second):
    count = lax.axis_size("rows")
    pairs = lambda start: [
        pair for i in range(start, count - 1, 2) for pair in ((i, i + 1), (i + 1, i))
    ]
    got_second = lax.ppermute(second, "rows", pairs(1))
    got_first = lax.ppermute(first, "rows", pairs(0))
    return got_first, got_second


def share_over_hist(parts):
    count = lax.axis_size("hist")
    return [
        lax.ppermute(parts[shift - 1], "hist", [(i, (i + shift) % count) for i in range(count)])
        for shift in range(1, count)
    ]


def total_over(values, axes):
    for axis in axes:
        count = lax.axis_size(axis)
        if count & (count - 1):
            values = lax.psum(values, axis)
            continue
        span = 1
        while span < count:
            values = values + lax.ppermute(values, axis, [(i, i ^ span) for i in range(count)])
            span *= 2
    return values


def body(hists, log_scaling_fields, histogram_weight_list):
    masses = hists[0]
    logs = log_scaling_fields[0]
    height, width = masses.shape
    count = lax.axis_size("hist")
    edge = 2 * HALF
    inner = height - edge
    share = width // count
    wide = width + LANES
    matmul = 2 * height * width * 3 * 256

    sides = 1 if lax.axis_size("cols") == 2 else 2
    tiles = [(height, LANES)] * sides
    edges = call(functools.partial(edge_kernel, jnp.exp), "log_edges", (logs,), tiles)
    from_left, from_right = swap_columns(edges)
    (partial,) = call(spread_kernel, "spread", (logs,), [(height, wide)], [(height, width + LANES)], cost=matmul)
    across, first, second = call(
        spread_edge_kernel, "spread_edge", (partial, logs, from_left, from_right),
        [(height, wide), (HALF, wide), (HALF, wide)], cost=matmul // 8,
    )
    edges = call(functools.partial(edge_kernel, lambda x: x), "mass_edges", (masses, first), tiles)
    from_left, from_right = swap_columns(edges)
    first, second = swap_rows(first, second)
    (inside,) = call(
        inner_ratio_kernel, "inner_ratio", (across, masses, from_left, from_right),
        [(inner, width)], [(inner, wide), (inner, wide)], cost=matmul,
    )
    rims, first, second = call(
        rim_ratio_kernel, "rim_ratio",
        (inside, across, first, second, masses, from_left, from_right),
        [(edge, width), (HALF, width), (HALF, width)], [(edge, wide), (edge, wide)], cost=matmul,
    )
    first, second = swap_rows(first, second)

    weights = histogram_weight_list
    inner_smooth, inner_own, inner_first = call(
        inner_log_kernel, "inner_log", (weights, rims, inside, logs),
        [(inner, width), (inner, width), (count - 1, inner, share)], scalars=1, cost=matmul,
    )
    inner_first = share_over_hist(inner_first)
    rim_smooth, rim_own, rim_first = call(
        rim_log_kernel, "rim_log", (weights, first, second, rims, inside, logs),
        [(edge, width), (edge, width), (count - 1, edge, share)], scalars=1, cost=matmul,
    )
    rim_first = share_over_hist(rim_first)
    inner_mean, inner_change, mass, later = call(
        inner_mean_kernel, "inner_mean", (inner_own, inner_smooth, rim_own, *inner_first),
        [(inner, share), (inner, share), (8, LANES), (count - 1, height, width - share)], cost=matmul // 4,
    )
    later = share_over_hist(later)
    rim_mean, rim_change, mass = call(
        rim_mean_kernel, "rim_mean", (rim_own, rim_smooth, mass, *rim_first),
        [(edge, share), (edge, share), (8, LANES)], cost=10 * matmul,
    )
    mass = total_over(mass, ("cols", "rows", "hist"))
    later_mean, later_change = call(
        later_mean_kernel, "later_mean", (rim_own, rim_smooth, inner_own, inner_smooth, *later),
        [(height, width - share), (height, width - share)], cost=matmul // 4,
    )
    cells = height * lax.axis_size("rows") * width * lax.axis_size("cols")
    barycenter, new_logs = call(
        functools.partial(final_kernel, float(cells)), "final",
        (mass, rim_mean, rim_change, inner_mean, inner_change, later_mean, later_change),
        [(height, width), (height, width)], [(2, height, width)], far_out=True, sems=(2, count), cost=matmul // 4,
    )
    return (barycenter, new_logs[None])


def solution(mesh):
    return jax.shard_map(
        body,
        mesh=mesh,
        in_specs=(
            P("hist", ("groups", "rows"), "cols"),
            P("hist", ("groups", "rows"), "cols"),
            P(),
        ),
        out_specs=(P(("groups", "rows"), "cols"), P("hist", ("groups", "rows"), "cols")),
        check_vma=False,
    )
```

```python
import functools

import jax
import jax.numpy as jnp
import numpy as np
from jax import lax
from jax.experimental import pallas as pl
from jax.experimental.pallas import tpu as pltpu
from jax.sharding import PartitionSpec as P

HALF = 32
LANES = 128
kernel_sigma = 16.0


def taps_total():
    taps = np.arange(-HALF, HALF + 1).astype(np.float64)
    return float(np.sum(np.exp(-taps * taps / (2.0 * kernel_sigma * kernel_sigma))))


def band_matrix(shape, axis_in):
    places = lax.broadcasted_iota(jnp.int32, shape, axis_in) - lax.broadcasted_iota(jnp.int32, shape, 1 - axis_in)
    offsets = (places - HALF).astype(jnp.float32)
    entries = jnp.exp(-offsets * offsets / (2.0 * kernel_sigma * kernel_sigma)) / taps_total()
    return jnp.where(jnp.abs(offsets) <= HALF, entries, 0.0)


def bands_kernel(columns, inner, rim):
    high, low = split(band_matrix((LANES + 2 * HALF, LANES), 0))
    columns[...] = jnp.concatenate([high, low], axis=1)
    for rows in (inner, rim):
        count = rows.shape[0] // 2
        high, low = split(band_matrix((count, count + 2 * HALF), 1))
        rows[...] = jnp.concatenate(
            [jnp.concatenate([high, high], axis=1), jnp.concatenate([low, jnp.zeros_like(low)], axis=1)], axis=0
        )


def split(values):
    high = values.astype(jnp.bfloat16)
    low = (values - high.astype(jnp.float32)).astype(jnp.bfloat16)
    return high, low


def dot(left, right):
    return jnp.dot(left, right, preferred_element_type=jnp.float32)


def column_block(window, band):
    high, low = split(window)
    depth = window.shape[1]
    both = dot(high, band[:depth])
    return both[:, :LANES] + both[:, LANES:] + dot(low, band[:depth, :LANES])


def row_block(window, band):
    high, low = split(window)
    rows = band.shape[0] // 2
    both = dot(band, jnp.concatenate([high, low], axis=0))
    return both[:rows] + both[rows:]


def edge_flags():
    place = lax.axis_index("cols")
    return (place > 0).astype(jnp.float32), (place < lax.axis_size("cols") - 1).astype(jnp.float32)


def row_parity():
    return lax.rem(lax.axis_index("rows"), 2)


def chunks(width, step):
    return [(start, min(start + step, width)) for start in range(0, width, step)]


def edge_sides():
    return [lax.axis_index("cols") == 0] if lax.axis_size("cols") == 2 else [True, False]


def edge_tiles(values, outs):
    width = values.shape[1]
    for out, right in zip(outs, edge_sides()):
        start = pl.multiple_of(jnp.where(right, width - LANES, 0), LANES)
        out[...] = values[:, pl.ds(start, LANES)]


def log_edge_kernel(logs, taps, kept, *outs):
    edge_tiles(logs, outs)
    for out in outs:
        out[...] = jnp.exp(out[...])
    kept[...] = logs[...]


def half_sends(which, across, first, second):
    height, share = across.shape[0], first.shape[1] - LANES
    odd = row_parity()
    lanes = pl.ds(pl.multiple_of(half_place(which) * share, LANES), share + LANES)
    first[...] = across[pl.ds(pl.multiple_of((1 - odd) * (height - HALF), HALF), HALF), lanes]
    second[...] = across[pl.ds(pl.multiple_of(odd * (height - HALF), HALF), HALF), lanes]


def mass_edge_kernel(masses, across, after, first, second, *outs):
    half_sends("own", across, first, second)
    edge_tiles(masses, outs)


def spread_kernel(logs, taps, across, wide):
    width = logs.shape[1]
    edge = 2 * HALF
    wide[:, edge : edge + width] = jnp.exp(logs[...])
    for start in range(LANES, width, LANES):
        across[:, start : start + LANES] = column_block(wide[:, start : start + LANES + 2 * HALF], taps[...])


def spread_edge_kernel(partial, logs, from_left, from_right, taps, across, first, second):
    has_left, has_right = edge_flags()
    height, width = logs.shape
    edge = 2 * HALF
    across[...] = partial[...]
    left = jnp.concatenate([from_left[:, edge:] * has_left, jnp.exp(logs[:, :LANES])], axis=1)
    right = jnp.concatenate([jnp.exp(logs[:, width - edge :]), from_right[:, :edge] * has_right], axis=1)
    across[:, :LANES] = column_block(left, taps[...])
    across[:, width : width + LANES] = column_block(right, taps[...])
    half_sends("other", across, first, second)


def ratio_of(masses, smooth):
    return jnp.where(masses > 0.0, masses / smooth, 0.0)


def column_pass(ratios, taps, out):
    for start in range(0, out.shape[1], LANES):
        out[:, start : start + LANES] = column_block(ratios[:, start : start + LANES + 2 * HALF], taps[...])


def own_weight(weights):
    mine = lax.broadcasted_iota(jnp.int32, weights.shape, 1) == lax.axis_index("hist")
    own = jnp.sum(jnp.where(mine, weights[...], 0.0), axis=1, keepdims=True)
    return own / jnp.sum(weights[...], axis=1, keepdims=True)


def inner_ratio_kernel(
    across, masses, from_left, from_right, weights, taps, row_taps, out, wide, weight, smooth, ratios
):
    weight[...] = jnp.broadcast_to(own_weight(weights), weight.shape)
    has_left, has_right = edge_flags()
    height = masses.shape[0]
    wide[...] = jnp.concatenate(
        [
            from_left[:, LANES - HALF :] * has_left,
            masses[...],
            from_right[:, :HALF] * has_right,
            jnp.zeros((height, 2 * HALF), jnp.float32),
        ],
        axis=1,
    )
    for start, stop in chunks(across.shape[1], 256):
        smooth[:, start:stop] = row_block(across[:, start:stop], row_taps[...])
    ratios[...] = ratio_of(wide[HALF : height - HALF, :], smooth[...])
    column_pass(ratios, taps, out)


def half_place(which):
    place = lax.axis_index("hist") if lax.axis_size("hist") == 2 else 0
    return 1 - place if which == "other" else place


def rim_ratio_kernel(
    which, across, first, second, wide, taps, row_taps, after, rims, sent_first, sent_second, smooth, ratios
):
    height = across.shape[0]
    share = rims.shape[1]
    odd = row_parity()
    offset = half_place(which) * share
    for start, stop in chunks(share + LANES, 256):
        lanes = pl.ds(pl.multiple_of(offset + start, LANES), stop - start)
        one, two = first[:, start:stop], second[:, start:stop]
        upper = jnp.concatenate([jnp.where(odd == 1, one, two), across[: 2 * HALF, lanes]], axis=0)
        lower = jnp.concatenate([across[height - 2 * HALF :, lanes], jnp.where(odd == 1, two, one)], axis=0)
        smooth[:HALF, start:stop] = row_block(upper, row_taps[...])
        smooth[HALF:, start:stop] = row_block(lower, row_taps[...])
    lanes = pl.ds(pl.multiple_of(offset, LANES), share + LANES)
    masses = jnp.concatenate([wide[:HALF, lanes], wide[height - HALF :, lanes]], axis=0)
    ratios[...] = ratio_of(masses, smooth[...])
    column_pass(ratios, taps, rims)
    sent_first[...] = rims[pl.ds(pl.multiple_of((1 - odd) * HALF, HALF), HALF), :]
    sent_second[...] = rims[pl.ds(pl.multiple_of(odd * HALF, HALF), HALF), :]


def inner_log_kernel(which, weight, rims, inner, logs, row_taps, smooth, own):
    height = logs.shape[0]
    share = rims.shape[1]
    offset = half_place(which) * share
    for start, stop in chunks(share, 256):
        lanes = pl.ds(pl.multiple_of(offset + start, LANES), stop - start)
        window = jnp.concatenate([rims[:HALF, start:stop], inner[:, lanes], rims[HALF:, start:stop]], axis=0)
        smooth[:, start:stop] = jnp.log(row_block(window, row_taps[...]))
    lanes = pl.ds(pl.multiple_of(offset, LANES), share)
    own[...] = weight[:1, :1] * (logs[HALF : height - HALF, lanes] + smooth[...])


def rim_log_kernel(which, weight, from_first, from_second, rims, inner, logs, row_taps, after, smooth, own):
    height = logs.shape[0]
    depth = inner.shape[0]
    share = rims.shape[1]
    odd = row_parity()
    offset = half_place(which) * share
    for start, stop in chunks(share, 256):
        lanes = pl.ds(pl.multiple_of(offset + start, LANES), stop - start)
        one, two = from_first[:, start:stop], from_second[:, start:stop]
        above, below = jnp.where(odd == 1, one, two), jnp.where(odd == 1, two, one)
        upper = jnp.concatenate([above, rims[:HALF, start:stop], inner[:HALF, lanes]], axis=0)
        lower = jnp.concatenate([inner[depth - HALF :, lanes], rims[HALF:, start:stop], below], axis=0)
        smooth[:HALF, start:stop] = jnp.log(row_block(upper, row_taps[...]))
        smooth[HALF:, start:stop] = jnp.log(row_block(lower, row_taps[...]))
    lanes = pl.ds(pl.multiple_of(offset, LANES), share)
    log_rows = jnp.concatenate([logs[:HALF, lanes], logs[height - HALF :, lanes]], axis=0)
    own[...] = weight[:1, :1] * (log_rows + smooth[...])


def folded(values):
    rows, width = values.shape
    total = jnp.sum(values.reshape(rows // 8, 8, width), axis=0)
    return sum(total[:, start : start + LANES] for start in range(0, width, LANES))


def mean_part(own, smooth, arrived, mean, change):
    log_mean = own[...] + arrived[...]
    values = jnp.exp(log_mean)
    mean[...] = values
    change[...] = log_mean - smooth[...]
    return folded(values)


def inner_mean_kernel(own, smooth, arrived, mean, change, partial):
    partial[...] = mean_part(own, smooth, arrived, mean, change)


def rim_mean_kernel(own, smooth, arrived, inner_own, before, mean, change, partial, later):
    partial[...] = before[...] + mean_part(own, smooth, arrived, mean, change)
    height = later.shape[0]
    later[:HALF, :] = own[:HALF, :]
    later[HALF : height - HALF, :] = inner_own[...]
    later[height - HALF :, :] = own[HALF:, :]


def later_mean_kernel(rim_own, rim_smooth, inner_own, inner_smooth, arrived, mean, change):
    height = mean.shape[0]
    for rows, own, smooth, part in (
        (slice(0, HALF), rim_own, rim_smooth, slice(0, HALF)),
        (slice(HALF, height - HALF), inner_own, inner_smooth, slice(None)),
        (slice(height - HALF, height), rim_own, rim_smooth, slice(HALF, 2 * HALF)),
    ):
        log_mean = own[part, :] + arrived[rows, :]
        mean[rows, :] = jnp.exp(log_mean)
        change[rows, :] = log_mean - smooth[part, :]


def final_kernel(
    cells, total, rim_mean, rim_change, inner_mean, inner_change, later_mean, later_change, barycenter, new_logs,
    stage, sems,
):
    height, width = barycenter.shape
    share = width // 2
    scale = cells / jnp.sum(total[...], axis=(0, 1), keepdims=True)
    log_scale = jnp.log(scale)
    copies = []
    for k, (out, rim, inner, later, apply) in enumerate(
        (
            (barycenter, rim_mean, inner_mean, later_mean, lambda x: x * scale),
            (new_logs, rim_change, inner_change, later_change, lambda x: x + log_scale),
        )
    ):
        for step, which in enumerate(("own", "other")):
            slot = slice(step * share, (step + 1) * share)
            if which == "own":
                stage[k, :HALF, slot] = apply(rim[:HALF, :])
                stage[k, HALF : height - HALF, slot] = apply(inner[...])
                stage[k, height - HALF :, slot] = apply(rim[HALF:, :])
            else:
                stage[k, :, slot] = apply(later[...])
            lanes = pl.ds(pl.multiple_of(half_place(which) * share, LANES), share)
            copy = pltpu.make_async_copy(stage.at[k, :, slot], out.at[:, lanes], sems.at[k, step])
            copy.start()
            copies.append(copy)
    for copy in copies:
        copy.wait()


def call(kernel, name, args, outs, scratch=(), cost=0, far_out=False, sems=None):
    shaped = lambda shape: shape if isinstance(shape, jax.ShapeDtypeStruct) else jax.ShapeDtypeStruct(shape, jnp.float32)
    near = pl.BlockSpec(memory_space=pltpu.VMEM)
    far = pl.BlockSpec(memory_space=pl.ANY)
    return pl.pallas_call(
        kernel,
        name=name,
        out_shape=tuple(shaped(shape) for shape in outs),
        in_specs=[near for _ in args],
        out_specs=tuple(far if far_out else near for _ in outs),
        scratch_shapes=[pltpu.VMEM(shape, jnp.float32) for shape in scratch]
        + ([pltpu.SemaphoreType.DMA(sems)] if sems else []),
        compiler_params=pltpu.CompilerParams(vmem_limit_bytes=32 * 1024 * 1024),
        cost_estimate=pl.CostEstimate(flops=5 * cost, bytes_accessed=cost // 256, transcendentals=0),
    )(*args)


def swap_columns(edges):
    count = lax.axis_size("cols")
    if count == 2:
        got = lax.ppermute(edges[0], "cols", [(0, 1), (1, 0)])
        return got, got
    steps = [(i, i + 1) for i in range(count - 1)]
    right_edge, left_edge = edges
    return (
        lax.ppermute(right_edge, "cols", steps),
        lax.ppermute(left_edge, "cols", [(b, a) for a, b in steps]),
    )


def swap_rows(first, second):
    count = lax.axis_size("rows")
    pairs = lambda start: [
        pair for i in range(start, count - 1, 2) for pair in ((i, i + 1), (i + 1, i))
    ]
    got_second = lax.ppermute(second, "rows", pairs(1))
    got_first = lax.ppermute(first, "rows", pairs(0))
    return got_first, got_second


def swap_hist(values):
    return lax.ppermute(values, "hist", [(0, 1), (1, 0)])


def total_over(values, axes):
    for axis in axes:
        count = lax.axis_size(axis)
        if count & (count - 1):
            values = lax.psum(values, axis)
            continue
        span = 1
        while span < count:
            values = values + lax.ppermute(values, axis, [(i, i ^ span) for i in range(count)])
            span *= 2
    return values


def body(hists, log_scaling_fields, histogram_weight_list):
    masses = hists[0]
    logs = log_scaling_fields[0]
    weights = histogram_weight_list
    height, width = masses.shape
    count = lax.axis_size("hist")
    edge = 2 * HALF
    inner = height - edge
    share = width // 2
    wide_width = width + LANES
    matmul = 2 * height * width * 3 * 256
    cells = height * lax.axis_size("rows") * width * lax.axis_size("cols")

    half = lambda *shape: jax.ShapeDtypeStruct(shape, jnp.bfloat16)
    taps, inner_taps, rim_taps = call(
        bands_kernel, "bands", (),
        [half(LANES + edge, 2 * LANES), half(2 * inner, 2 * height), half(edge, 2 * (HALF + edge))],
    )
    sides = 1 if lax.axis_size("cols") == 2 else 2
    tiles = [(height, LANES)] * sides
    logs, *edges = call(log_edge_kernel, "log_edges", (logs, taps), [(height, width)] + tiles)
    from_left, from_right = swap_columns(edges)
    (partial,) = call(
        spread_kernel, "spread", (logs, taps), [(height, wide_width)], [(height, wide_width)], cost=matmul
    )
    across, *other_sent = call(
        spread_edge_kernel, "spread_edge", (partial, logs, from_left, from_right, taps),
        [(height, wide_width)] + [(HALF, share + LANES)] * 2, cost=matmul // 8,
    )
    first, second, *edges = call(
        mass_edge_kernel, "mass_edges", (masses, across, other_sent[0]), [(HALF, share + LANES)] * 2 + tiles,
        cost=20 * matmul,
    )
    own_sent = (first, second)
    from_left, from_right = swap_columns(edges)
    other_arrived = swap_rows(*other_sent)
    own_arrived = swap_rows(*own_sent)
    inside, masses, weight = call(
        inner_ratio_kernel, "inner_ratio",
        (across, masses, from_left, from_right, weights.reshape(1, count), taps, inner_taps),
        [(inner, width), (height, wide_width), (8, LANES)], [(inner, wide_width), (inner, wide_width)],
    )

    def rim_ratio(which, arrived, after):
        return call(
            functools.partial(rim_ratio_kernel, which), which + "_rim_ratio",
            (across, *arrived, masses, taps, rim_taps, after),
            [(edge, share), (HALF, share), (HALF, share)], [(edge, share + LANES)] * 2, cost=matmul,
        )

    def inner_log(which, rims):
        return call(
            functools.partial(inner_log_kernel, which), which + "_inner_log",
            (weight, rims, inside, logs, inner_taps), [(inner, share)] * 2, cost=matmul,
        )

    def rim_log(which, rims, arrived, after):
        return call(
            functools.partial(rim_log_kernel, which), which + "_rim_log",
            (weight, *arrived, rims, inside, logs, rim_taps, after), [(edge, share)] * 2, cost=matmul,
        )

    other_rims, *sent = rim_ratio("other", other_arrived, inside)
    other_arrived = swap_rows(*sent)
    other_inner_smooth, other_inner_own = inner_log("other", other_rims)
    own_rims, *sent = rim_ratio("own", own_arrived, other_inner_own)
    own_arrived = swap_rows(*sent)
    other_rim_smooth, other_rim_own = rim_log("other", other_rims, other_arrived, own_rims)
    inner_smooth, inner_own = inner_log("own", own_rims)
    rim_smooth, rim_own = rim_log("own", own_rims, own_arrived, other_rim_own)

    if count != 2:
        joined = lambda rim, inside: jnp.concatenate([rim[:HALF], inside, rim[HALF:]], axis=0)
        both = lambda *parts: jnp.concatenate([joined(*parts[:2]), joined(*parts[2:])], axis=1)
        log_mean = lax.psum(both(rim_own, inner_own, other_rim_own, other_inner_own), "hist")
        log_smooth = both(rim_smooth, inner_smooth, other_rim_smooth, other_inner_smooth)
        mean = jnp.exp(log_mean)
        scale = cells / lax.psum(jnp.sum(mean), ("rows", "cols"))
        return (mean * scale, (log_mean + jnp.log(scale) - log_smooth)[None])

    inner_arrived = swap_hist(other_inner_own)
    rim_arrived = swap_hist(other_rim_own)
    inner_mean, inner_change, mass = call(
        inner_mean_kernel, "inner_mean", (inner_own, inner_smooth, inner_arrived),
        [(inner, share), (inner, share), (8, LANES)], cost=matmul // 4,
    )
    rim_mean, rim_change, mass, later = call(
        rim_mean_kernel, "rim_mean", (rim_own, rim_smooth, rim_arrived, inner_own, mass),
        [(edge, share), (edge, share), (8, LANES), (height, share)], cost=matmul // 4,
    )
    later_arrived = swap_hist(later)
    mass = total_over(mass, ("cols", "rows", "hist"))
    later_mean, later_change = call(
        later_mean_kernel, "later_mean",
        (other_rim_own, other_rim_smooth, other_inner_own, other_inner_smooth, later_arrived),
        [(height, share)] * 2, cost=matmul // 4,
    )
    barycenter, new_logs = call(
        functools.partial(final_kernel, float(cells)), "final",
        (mass, rim_mean, rim_change, inner_mean, inner_change, later_mean, later_change),
        [(height, width)] * 2, [(2, height, width)], far_out=True, sems=(2, 2), cost=matmul // 4,
    )
    return (barycenter, new_logs[None])


def solution(mesh):
    return jax.shard_map(
        body,
        mesh=mesh,
        in_specs=(
            P("hist", ("groups", "rows"), "cols"),
            P("hist", ("groups", "rows"), "cols"),
            P(),
        ),
        out_specs=(P(("groups", "rows"), "cols"), P("hist", ("groups", "rows"), "cols")),
        check_vma=False,
    )
```

```python
import functools

import jax
import jax.numpy as jnp
import numpy as np
from jax import lax
from jax.experimental import pallas as pl
from jax.experimental.pallas import tpu as pltpu
from jax.sharding import PartitionSpec as P

HALF = 32
LANES = 128
kernel_sigma = 16.0


def taps_total():
    taps = np.arange(-HALF, HALF + 1).astype(np.float64)
    return float(np.sum(np.exp(-taps * taps / (2.0 * kernel_sigma * kernel_sigma))))


def band_matrix(shape, axis_in):
    places = lax.broadcasted_iota(jnp.int32, shape, axis_in) - lax.broadcasted_iota(jnp.int32, shape, 1 - axis_in)
    offsets = (places - HALF).astype(jnp.float32)
    entries = jnp.exp(-offsets * offsets / (2.0 * kernel_sigma * kernel_sigma)) / taps_total()
    return jnp.where(jnp.abs(offsets) <= HALF, entries, 0.0)


def bands_kernel(columns, inner, rim):
    high, low = split(band_matrix((LANES + 2 * HALF, LANES), 0))
    columns[...] = jnp.concatenate([high, low], axis=1)
    for rows in (inner, rim):
        count = rows.shape[0] // 2
        high, low = split(band_matrix((count, count + 2 * HALF), 1))
        rows[...] = jnp.concatenate(
            [jnp.concatenate([high, high], axis=1), jnp.concatenate([low, jnp.zeros_like(low)], axis=1)], axis=0
        )


def split(values):
    high = values.astype(jnp.bfloat16)
    low = (values - high.astype(jnp.float32)).astype(jnp.bfloat16)
    return high, low


def dot(left, right):
    return jnp.dot(left, right, preferred_element_type=jnp.float32)


def column_block(window, band):
    high, low = split(window)
    depth = window.shape[1]
    both = dot(high, band[:depth])
    return both[:, :LANES] + both[:, LANES:] + dot(low, band[:depth, :LANES])


def row_block(window, band):
    high, low = split(window)
    rows = band.shape[0] // 2
    both = dot(band, jnp.concatenate([high, low], axis=0))
    return both[:rows] + both[rows:]


def edge_flags():
    place = lax.axis_index("cols")
    return (place > 0).astype(jnp.float32), (place < lax.axis_size("cols") - 1).astype(jnp.float32)


def row_parity(flip):
    return lax.rem(lax.axis_index("rows") + flip, 2)


def chunks(width, step):
    return [(start, min(start + step, width)) for start in range(0, width, step)]


def edge_sides():
    return [lax.axis_index("cols") == 0] if lax.axis_size("cols") == 2 else [True, False]


def edge_tiles(values, outs):
    width = values.shape[1]
    for out, right in zip(outs, edge_sides()):
        start = pl.multiple_of(jnp.where(right, width - LANES, 0), LANES)
        out[...] = values[:, pl.ds(start, LANES)]


def log_edge_kernel(logs, taps, kept, *outs):
    edge_tiles(logs, outs)
    for out in outs:
        out[...] = jnp.exp(out[...])
    kept[...] = logs[...]


def half_sends(which, flip, across, first, second):
    height, share = across.shape[0], first.shape[1] - LANES
    odd = row_parity(flip)
    lanes = pl.ds(pl.multiple_of(half_place(which) * share, LANES), share + LANES)
    first[...] = across[pl.ds(pl.multiple_of((1 - odd) * (height - HALF), HALF), HALF), lanes]
    second[...] = across[pl.ds(pl.multiple_of(odd * (height - HALF), HALF), HALF), lanes]


def mass_edge_kernel(masses, across, after, first, second, *outs):
    half_sends("own", 1, across, first, second)
    edge_tiles(masses, outs)


def spread_kernel(logs, taps, across, wide):
    width = logs.shape[1]
    edge = 2 * HALF
    wide[:, edge : edge + width] = jnp.exp(logs[...])
    for start in range(LANES, width, LANES):
        across[:, start : start + LANES] = column_block(wide[:, start : start + LANES + 2 * HALF], taps[...])


def spread_edge_kernel(partial, logs, from_left, from_right, taps, across, first, second):
    has_left, has_right = edge_flags()
    height, width = logs.shape
    edge = 2 * HALF
    across[...] = partial[...]
    left = jnp.concatenate([from_left[:, edge:] * has_left, jnp.exp(logs[:, :LANES])], axis=1)
    right = jnp.concatenate([jnp.exp(logs[:, width - edge :]), from_right[:, :edge] * has_right], axis=1)
    across[:, :LANES] = column_block(left, taps[...])
    across[:, width : width + LANES] = column_block(right, taps[...])
    half_sends("other", 0, across, first, second)


def ratio_of(masses, smooth):
    return jnp.where(masses > 0.0, masses / smooth, 0.0)


def column_pass(ratios, taps, out):
    for start in range(0, out.shape[1], LANES):
        out[:, start : start + LANES] = column_block(ratios[:, start : start + LANES + 2 * HALF], taps[...])


def own_weight(weights):
    mine = lax.broadcasted_iota(jnp.int32, weights.shape, 1) == lax.axis_index("hist")
    own = jnp.sum(jnp.where(mine, weights[...], 0.0), axis=1, keepdims=True)
    return own / jnp.sum(weights[...], axis=1, keepdims=True)


def inner_ratio_kernel(
    across, masses, from_left, from_right, weights, taps, row_taps, out, wide, weight, smooth, ratios
):
    weight[...] = jnp.broadcast_to(own_weight(weights), weight.shape)
    has_left, has_right = edge_flags()
    height = masses.shape[0]
    wide[...] = jnp.concatenate(
        [
            from_left[:, LANES - HALF :] * has_left,
            masses[...],
            from_right[:, :HALF] * has_right,
            jnp.zeros((height, 2 * HALF), jnp.float32),
        ],
        axis=1,
    )
    for start, stop in chunks(across.shape[1], 256):
        smooth[:, start:stop] = row_block(across[:, start:stop], row_taps[...])
    ratios[...] = ratio_of(wide[HALF : height - HALF, :], smooth[...])
    column_pass(ratios, taps, out)


def half_place(which):
    place = lax.axis_index("hist") if lax.axis_size("hist") == 2 else 0
    return 1 - place if which == "other" else place


def rim_ratio_kernel(
    which, came, goes, across, first, second, wide, taps, row_taps, after, rims, sent_first, sent_second, smooth, ratios
):
    height = across.shape[0]
    share = rims.shape[1]
    odd = row_parity(came)
    offset = half_place(which) * share
    for start, stop in chunks(share + LANES, 256):
        lanes = pl.ds(pl.multiple_of(offset + start, LANES), stop - start)
        one, two = first[:, start:stop], second[:, start:stop]
        upper = jnp.concatenate([jnp.where(odd == 1, one, two), across[: 2 * HALF, lanes]], axis=0)
        lower = jnp.concatenate([across[height - 2 * HALF :, lanes], jnp.where(odd == 1, two, one)], axis=0)
        smooth[:HALF, start:stop] = row_block(upper, row_taps[...])
        smooth[HALF:, start:stop] = row_block(lower, row_taps[...])
    lanes = pl.ds(pl.multiple_of(offset, LANES), share + LANES)
    masses = jnp.concatenate([wide[:HALF, lanes], wide[height - HALF :, lanes]], axis=0)
    ratios[...] = ratio_of(masses, smooth[...])
    column_pass(ratios, taps, rims)
    odd = row_parity(goes)
    sent_first[...] = rims[pl.ds(pl.multiple_of((1 - odd) * HALF, HALF), HALF), :]
    sent_second[...] = rims[pl.ds(pl.multiple_of(odd * HALF, HALF), HALF), :]


def inner_log_kernel(which, weight, rims, inner, logs, row_taps, smooth, own):
    height = logs.shape[0]
    share = rims.shape[1]
    offset = half_place(which) * share
    for start, stop in chunks(share, 256):
        lanes = pl.ds(pl.multiple_of(offset + start, LANES), stop - start)
        window = jnp.concatenate([rims[:HALF, start:stop], inner[:, lanes], rims[HALF:, start:stop]], axis=0)
        smooth[:, start:stop] = jnp.log(row_block(window, row_taps[...]))
    lanes = pl.ds(pl.multiple_of(offset, LANES), share)
    own[...] = weight[:1, :1] * (logs[HALF : height - HALF, lanes] + smooth[...])


def rim_log_kernel(which, came, weight, from_first, from_second, rims, inner, logs, row_taps, after, smooth, own):
    height = logs.shape[0]
    depth = inner.shape[0]
    share = rims.shape[1]
    odd = row_parity(came)
    offset = half_place(which) * share
    for start, stop in chunks(share, 256):
        lanes = pl.ds(pl.multiple_of(offset + start, LANES), stop - start)
        one, two = from_first[:, start:stop], from_second[:, start:stop]
        above, below = jnp.where(odd == 1, one, two), jnp.where(odd == 1, two, one)
        upper = jnp.concatenate([above, rims[:HALF, start:stop], inner[:HALF, lanes]], axis=0)
        lower = jnp.concatenate([inner[depth - HALF :, lanes], rims[HALF:, start:stop], below], axis=0)
        smooth[:HALF, start:stop] = jnp.log(row_block(upper, row_taps[...]))
        smooth[HALF:, start:stop] = jnp.log(row_block(lower, row_taps[...]))
    lanes = pl.ds(pl.multiple_of(offset, LANES), share)
    log_rows = jnp.concatenate([logs[:HALF, lanes], logs[height - HALF :, lanes]], axis=0)
    own[...] = weight[:1, :1] * (log_rows + smooth[...])


def folded(values):
    rows, width = values.shape
    total = jnp.sum(values.reshape(rows // 8, 8, width), axis=0)
    return sum(total[:, start : start + LANES] for start in range(0, width, LANES))


def mean_part(own, smooth, arrived, mean, change):
    log_mean = own[...] + arrived[...]
    values = jnp.exp(log_mean)
    mean[...] = values
    change[...] = log_mean - smooth[...]
    return folded(values)


def inner_mean_kernel(own, smooth, arrived, mean, change, partial):
    partial[...] = mean_part(own, smooth, arrived, mean, change)


def rim_mean_kernel(own, smooth, arrived, inner_own, before, mean, change, partial, later):
    partial[...] = before[...] + mean_part(own, smooth, arrived, mean, change)
    height = later.shape[0]
    later[:HALF, :] = own[:HALF, :]
    later[HALF : height - HALF, :] = inner_own[...]
    later[height - HALF :, :] = own[HALF:, :]


def later_mean_kernel(rim_own, rim_smooth, inner_own, inner_smooth, arrived, mean, change):
    height = mean.shape[0]
    for rows, own, smooth, part in (
        (slice(0, HALF), rim_own, rim_smooth, slice(0, HALF)),
        (slice(HALF, height - HALF), inner_own, inner_smooth, slice(None)),
        (slice(height - HALF, height), rim_own, rim_smooth, slice(HALF, 2 * HALF)),
    ):
        log_mean = own[part, :] + arrived[rows, :]
        mean[rows, :] = jnp.exp(log_mean)
        change[rows, :] = log_mean - smooth[part, :]


def final_kernel(
    cells, total, rim_mean, rim_change, inner_mean, inner_change, later_mean, later_change, barycenter, new_logs,
    stage, sems,
):
    height, width = barycenter.shape
    share = width // 2
    scale = cells / jnp.sum(total[...], axis=(0, 1), keepdims=True)
    log_scale = jnp.log(scale)
    copies = []
    for k, (out, rim, inner, later, apply) in enumerate(
        (
            (barycenter, rim_mean, inner_mean, later_mean, lambda x: x * scale),
            (new_logs, rim_change, inner_change, later_change, lambda x: x + log_scale),
        )
    ):
        for step, which in enumerate(("own", "other")):
            slot = slice(step * share, (step + 1) * share)
            if which == "own":
                stage[k, :HALF, slot] = apply(rim[:HALF, :])
                stage[k, HALF : height - HALF, slot] = apply(inner[...])
                stage[k, height - HALF :, slot] = apply(rim[HALF:, :])
            else:
                stage[k, :, slot] = apply(later[...])
            lanes = pl.ds(pl.multiple_of(half_place(which) * share, LANES), share)
            copy = pltpu.make_async_copy(stage.at[k, :, slot], out.at[:, lanes], sems.at[k, step])
            copy.start()
            copies.append(copy)
    for copy in copies:
        copy.wait()


def call(kernel, name, args, outs, scratch=(), cost=0, far_out=False, sems=None):
    shaped = lambda shape: shape if isinstance(shape, jax.ShapeDtypeStruct) else jax.ShapeDtypeStruct(shape, jnp.float32)
    near = pl.BlockSpec(memory_space=pltpu.VMEM)
    far = pl.BlockSpec(memory_space=pl.ANY)
    return pl.pallas_call(
        kernel,
        name=name,
        out_shape=tuple(shaped(shape) for shape in outs),
        in_specs=[near for _ in args],
        out_specs=tuple(far if far_out else near for _ in outs),
        scratch_shapes=[pltpu.VMEM(shape, jnp.float32) for shape in scratch]
        + ([pltpu.SemaphoreType.DMA(sems)] if sems else []),
        compiler_params=pltpu.CompilerParams(vmem_limit_bytes=32 * 1024 * 1024),
        cost_estimate=pl.CostEstimate(flops=5 * cost, bytes_accessed=cost // 256, transcendentals=0),
    )(*args)


def swap_columns(edges):
    count = lax.axis_size("cols")
    if count == 2:
        got = lax.ppermute(edges[0], "cols", [(0, 1), (1, 0)])
        return got, got
    steps = [(i, i + 1) for i in range(count - 1)]
    right_edge, left_edge = edges
    return (
        lax.ppermute(right_edge, "cols", steps),
        lax.ppermute(left_edge, "cols", [(b, a) for a, b in steps]),
    )


def swap_rows(flip, first, second):
    count = lax.axis_size("rows")
    pairs = lambda start: [
        pair for i in range(start, count - 1, 2) for pair in ((i, i + 1), (i + 1, i))
    ]
    return lax.ppermute(first, "rows", pairs(flip)), lax.ppermute(second, "rows", pairs(1 - flip))


def swap_hist(values):
    return lax.ppermute(values, "hist", [(0, 1), (1, 0)])


def total_over(values, axes):
    count = lax.axis_size(axes)
    if count & (count - 1):
        return lax.psum(values, axes)
    arrived = [lax.ppermute(values, axes, [(i, i ^ mask) for i in range(count)]) for mask in range(1, count)]
    return values + sum(arrived)


def body(hists, log_scaling_fields, histogram_weight_list):
    masses = hists[0]
    logs = log_scaling_fields[0]
    weights = histogram_weight_list
    height, width = masses.shape
    count = lax.axis_size("hist")
    edge = 2 * HALF
    inner = height - edge
    share = width // 2
    wide_width = width + LANES
    matmul = 2 * height * width * 3 * 256
    cells = height * lax.axis_size("rows") * width * lax.axis_size("cols")

    half = lambda *shape: jax.ShapeDtypeStruct(shape, jnp.bfloat16)
    taps, inner_taps, rim_taps = call(
        bands_kernel, "bands", (),
        [half(LANES + edge, 2 * LANES), half(2 * inner, 2 * height), half(edge, 2 * (HALF + edge))],
    )
    flips = {"other": (0, 0), "own": (1, 0)}
    sides = 1 if lax.axis_size("cols") == 2 else 2
    tiles = [(height, LANES)] * sides
    logs, *edges = call(log_edge_kernel, "log_edges", (logs, taps), [(height, width)] + tiles)
    from_left, from_right = swap_columns(edges)
    (partial,) = call(
        spread_kernel, "spread", (logs, taps), [(height, wide_width)], [(height, wide_width)], cost=matmul
    )
    across, *other_sent = call(
        spread_edge_kernel, "spread_edge", (partial, logs, from_left, from_right, taps),
        [(height, wide_width)] + [(HALF, share + LANES)] * 2, cost=matmul // 8,
    )
    first, second, *edges = call(
        mass_edge_kernel, "mass_edges", (masses, across, other_sent[0]), [(HALF, share + LANES)] * 2 + tiles,
        cost=20 * matmul,
    )
    own_sent = (first, second)
    from_left, from_right = swap_columns(edges)
    other_arrived = swap_rows(0, *other_sent)
    own_arrived = swap_rows(1, *own_sent)
    inside, masses, weight = call(
        inner_ratio_kernel, "inner_ratio",
        (across, masses, from_left, from_right, weights.reshape(1, count), taps, inner_taps),
        [(inner, width), (height, wide_width), (8, LANES)], [(inner, wide_width), (inner, wide_width)],
    )

    def rim_ratio(which, arrived, after):
        return call(
            functools.partial(rim_ratio_kernel, which, *flips[which]), which + "_rim_ratio",
            (across, *arrived, masses, taps, rim_taps, after),
            [(edge, share), (HALF, share), (HALF, share)], [(edge, share + LANES)] * 2, cost=matmul,
        )

    def inner_log(which, rims):
        return call(
            functools.partial(inner_log_kernel, which), which + "_inner_log",
            (weight, rims, inside, logs, inner_taps), [(inner, share)] * 2, cost=matmul,
        )

    def rim_log(which, rims, arrived, after):
        return call(
            functools.partial(rim_log_kernel, which, flips[which][1]), which + "_rim_log",
            (weight, *arrived, rims, inside, logs, rim_taps, after), [(edge, share)] * 2, cost=matmul,
        )

    other_rims, *sent = rim_ratio("other", other_arrived, inside)
    other_arrived = swap_rows(0, *sent)
    other_inner_smooth, other_inner_own = inner_log("other", other_rims)
    own_rims, *sent = rim_ratio("own", own_arrived, other_inner_own)
    own_arrived = swap_rows(0, *sent)
    other_rim_smooth, other_rim_own = rim_log("other", other_rims, other_arrived, own_rims)
    inner_smooth, inner_own = inner_log("own", own_rims)
    rim_smooth, rim_own = rim_log("own", own_rims, own_arrived, other_rim_own)

    if count != 2:
        joined = lambda rim, inside: jnp.concatenate([rim[:HALF], inside, rim[HALF:]], axis=0)
        both = lambda *parts: jnp.concatenate([joined(*parts[:2]), joined(*parts[2:])], axis=1)
        log_mean = lax.psum(both(rim_own, inner_own, other_rim_own, other_inner_own), "hist")
        log_smooth = both(rim_smooth, inner_smooth, other_rim_smooth, other_inner_smooth)
        mean = jnp.exp(log_mean)
        scale = cells / lax.psum(jnp.sum(mean), ("rows", "cols"))
        return (mean * scale, (log_mean + jnp.log(scale) - log_smooth)[None])

    inner_arrived = swap_hist(other_inner_own)
    rim_arrived = swap_hist(other_rim_own)
    inner_mean, inner_change, mass = call(
        inner_mean_kernel, "inner_mean", (inner_own, inner_smooth, inner_arrived),
        [(inner, share), (inner, share), (8, LANES)], cost=matmul // 4,
    )
    rim_mean, rim_change, mass, later = call(
        rim_mean_kernel, "rim_mean", (rim_own, rim_smooth, rim_arrived, inner_own, mass),
        [(edge, share), (edge, share), (8, LANES), (height, share)], cost=matmul // 4,
    )
    later_arrived = swap_hist(later)
    mass = total_over(mass, ("rows",))
    mass = total_over(mass, ("hist", "cols"))
    later_mean, later_change = call(
        later_mean_kernel, "later_mean",
        (other_rim_own, other_rim_smooth, other_inner_own, other_inner_smooth, later_arrived),
        [(height, share)] * 2, cost=matmul // 4,
    )
    barycenter, new_logs = call(
        functools.partial(final_kernel, float(cells)), "final",
        (mass, rim_mean, rim_change, inner_mean, inner_change, later_mean, later_change),
        [(height, width)] * 2, [(2, height, width)], far_out=True, sems=(2, 2), cost=matmul // 4,
    )
    return (barycenter, new_logs[None])


def solution(mesh):
    return jax.shard_map(
        body,
        mesh=mesh,
        in_specs=(
            P("hist", ("groups", "rows"), "cols"),
            P("hist", ("groups", "rows"), "cols"),
            P(),
        ),
        out_specs=(P(("groups", "rows"), "cols"), P("hist", ("groups", "rows"), "cols")),
        check_vma=False,
    )
```

```python
import functools

import jax
import jax.numpy as jnp
import numpy as np
from jax import lax
from jax.experimental import pallas as pl
from jax.experimental.pallas import tpu as pltpu
from jax.sharding import PartitionSpec as P

HALF = 32
LANES = 128
kernel_sigma = 16.0


def taps_total():
    taps = np.arange(-HALF, HALF + 1).astype(np.float64)
    return float(np.sum(np.exp(-taps * taps / (2.0 * kernel_sigma * kernel_sigma))))


def band_matrix(shape, axis_in):
    places = lax.broadcasted_iota(jnp.int32, shape, axis_in) - lax.broadcasted_iota(jnp.int32, shape, 1 - axis_in)
    offsets = (places - HALF).astype(jnp.float32)
    entries = jnp.exp(-offsets * offsets / (2.0 * kernel_sigma * kernel_sigma)) / taps_total()
    return jnp.where(jnp.abs(offsets) <= HALF, entries, 0.0)


def bands_kernel(columns, inner, rim):
    high, low = split(band_matrix((LANES + 2 * HALF, LANES), 0))
    columns[...] = jnp.concatenate([high, low], axis=1)
    for rows in (inner, rim):
        count = rows.shape[0] // 2
        high, low = split(band_matrix((count, count + 2 * HALF), 1))
        rows[...] = jnp.concatenate(
            [jnp.concatenate([high, high], axis=1), jnp.concatenate([low, jnp.zeros_like(low)], axis=1)], axis=0
        )


def split(values):
    high = values.astype(jnp.bfloat16)
    low = (values - high.astype(jnp.float32)).astype(jnp.bfloat16)
    return high, low


def dot(left, right):
    return jnp.dot(left, right, preferred_element_type=jnp.float32)


def column_block(window, band):
    high, low = split(window)
    depth = window.shape[1]
    both = dot(high, band[:depth])
    return both[:, :LANES] + both[:, LANES:] + dot(low, band[:depth, :LANES])


def row_block(window, band):
    high, low = split(window)
    rows = band.shape[0] // 2
    both = dot(band, jnp.concatenate([high, low], axis=0))
    return both[:rows] + both[rows:]


def edge_flags():
    place = lax.axis_index("cols")
    return (place > 0).astype(jnp.float32), (place < lax.axis_size("cols") - 1).astype(jnp.float32)


def row_parity(flip):
    return lax.rem(lax.axis_index("rows") + flip, 2)


def chunks(width, step):
    return [(start, min(start + step, width)) for start in range(0, width, step)]


def edge_sides():
    return [lax.axis_index("cols") == 0] if lax.axis_size("cols") == 2 else [True, False]


def edge_tiles(values, outs):
    width = values.shape[1]
    for out, right in zip(outs, edge_sides()):
        start = pl.multiple_of(jnp.where(right, width - LANES, 0), LANES)
        out[...] = values[:, pl.ds(start, LANES)]


def log_edge_kernel(logs, taps, kept, *outs):
    edge_tiles(logs, outs)
    for out in outs:
        out[...] = jnp.exp(out[...])
    kept[...] = logs[...]


def half_sends(which, flip, across, first, second):
    height, share = across.shape[0], first.shape[1] - LANES
    odd = row_parity(flip)
    lanes = pl.ds(pl.multiple_of(half_place(which) * share, LANES), share + LANES)
    first[...] = across[pl.ds(pl.multiple_of((1 - odd) * (height - HALF), HALF), HALF), lanes]
    second[...] = across[pl.ds(pl.multiple_of(odd * (height - HALF), HALF), HALF), lanes]


def mass_edge_kernel(masses, across, after, first, second, *outs):
    half_sends("own", 1, across, first, second)
    edge_tiles(masses, outs)


def spread_kernel(logs, taps, across, wide):
    width = logs.shape[1]
    edge = 2 * HALF
    wide[:, edge : edge + width] = jnp.exp(logs[...])
    for start in range(LANES, width, LANES):
        across[:, start : start + LANES] = column_block(wide[:, start : start + LANES + 2 * HALF], taps[...])


def spread_edge_kernel(partial, logs, from_left, from_right, taps, across, first, second):
    has_left, has_right = edge_flags()
    height, width = logs.shape
    edge = 2 * HALF
    across[...] = partial[...]
    left = jnp.concatenate([from_left[:, edge:] * has_left, jnp.exp(logs[:, :LANES])], axis=1)
    right = jnp.concatenate([jnp.exp(logs[:, width - edge :]), from_right[:, :edge] * has_right], axis=1)
    across[:, :LANES] = column_block(left, taps[...])
    across[:, width : width + LANES] = column_block(right, taps[...])
    half_sends("other", 0, across, first, second)


def ratio_of(masses, smooth):
    return jnp.where(masses > 0.0, masses / smooth, 0.0)


def column_pass(ratios, taps, out):
    for start in range(0, out.shape[1], LANES):
        out[:, start : start + LANES] = column_block(ratios[:, start : start + LANES + 2 * HALF], taps[...])


def own_weight(weights):
    mine = lax.broadcasted_iota(jnp.int32, weights.shape, 1) == lax.axis_index("hist")
    own = jnp.sum(jnp.where(mine, weights[...], 0.0), axis=1, keepdims=True)
    return own / jnp.sum(weights[...], axis=1, keepdims=True)


def inner_ratio_kernel(
    across, masses, from_left, from_right, weights, taps, row_taps, out, wide, weight, smooth, ratios
):
    weight[...] = jnp.broadcast_to(own_weight(weights), weight.shape)
    has_left, has_right = edge_flags()
    height = masses.shape[0]
    wide[...] = jnp.concatenate(
        [
            from_left[:, LANES - HALF :] * has_left,
            masses[...],
            from_right[:, :HALF] * has_right,
            jnp.zeros((height, 2 * HALF), jnp.float32),
        ],
        axis=1,
    )
    for start, stop in chunks(across.shape[1], 256):
        smooth[:, start:stop] = row_block(across[:, start:stop], row_taps[...])
    ratios[...] = ratio_of(wide[HALF : height - HALF, :], smooth[...])
    column_pass(ratios, taps, out)


def half_place(which):
    place = lax.axis_index("hist") if lax.axis_size("hist") == 2 else 0
    return 1 - place if which == "other" else place


def rim_ratio_kernel(
    which, came, across, first, second, wide, taps, row_taps, after, rims, smooth, ratios
):
    height = across.shape[0]
    share = rims.shape[1]
    odd = row_parity(came)
    offset = half_place(which) * share
    for start, stop in chunks(share + LANES, 256):
        lanes = pl.ds(pl.multiple_of(offset + start, LANES), stop - start)
        one, two = first[:, start:stop], second[:, start:stop]
        upper = jnp.concatenate([jnp.where(odd == 1, one, two), across[: 2 * HALF, lanes]], axis=0)
        lower = jnp.concatenate([across[height - 2 * HALF :, lanes], jnp.where(odd == 1, two, one)], axis=0)
        smooth[:HALF, start:stop] = row_block(upper, row_taps[...])
        smooth[HALF:, start:stop] = row_block(lower, row_taps[...])
    lanes = pl.ds(pl.multiple_of(offset, LANES), share + LANES)
    masses = jnp.concatenate([wide[:HALF, lanes], wide[height - HALF :, lanes]], axis=0)
    ratios[...] = ratio_of(masses, smooth[...])
    column_pass(ratios, taps, rims)


def inner_log_kernel(which, weight, rims, inner, logs, row_taps, smooth, own):
    height = logs.shape[0]
    share = rims.shape[1]
    offset = half_place(which) * share
    for start, stop in chunks(share, 256):
        lanes = pl.ds(pl.multiple_of(offset + start, LANES), stop - start)
        window = jnp.concatenate([rims[:HALF, start:stop], inner[:, lanes], rims[HALF:, start:stop]], axis=0)
        smooth[:, start:stop] = jnp.log(row_block(window, row_taps[...]))
    lanes = pl.ds(pl.multiple_of(offset, LANES), share)
    own[...] = weight[:1, :1] * (logs[HALF : height - HALF, lanes] + smooth[...])


def rim_sends_kernel(goes, rims, after, sent_first, sent_second):
    odd = row_parity(goes)
    sent_first[...] = rims[pl.ds(pl.multiple_of((1 - odd) * HALF, HALF), HALF), :]
    sent_second[...] = rims[pl.ds(pl.multiple_of(odd * HALF, HALF), HALF), :]


def rim_log_kernel(which, came, weight, from_first, from_second, rims, inner, logs, row_taps, after, smooth, own):
    height = logs.shape[0]
    depth = inner.shape[0]
    share = rims.shape[1]
    odd = row_parity(came)
    offset = half_place(which) * share
    for start, stop in chunks(share, 256):
        lanes = pl.ds(pl.multiple_of(offset + start, LANES), stop - start)
        one, two = from_first[:, start:stop], from_second[:, start:stop]
        above, below = jnp.where(odd == 1, one, two), jnp.where(odd == 1, two, one)
        upper = jnp.concatenate([above, rims[:HALF, start:stop], inner[:HALF, lanes]], axis=0)
        lower = jnp.concatenate([inner[depth - HALF :, lanes], rims[HALF:, start:stop], below], axis=0)
        smooth[:HALF, start:stop] = jnp.log(row_block(upper, row_taps[...]))
        smooth[HALF:, start:stop] = jnp.log(row_block(lower, row_taps[...]))
    lanes = pl.ds(pl.multiple_of(offset, LANES), share)
    log_rows = jnp.concatenate([logs[:HALF, lanes], logs[height - HALF :, lanes]], axis=0)
    own[...] = weight[:1, :1] * (log_rows + smooth[...])


def folded(values):
    rows, width = values.shape
    total = jnp.sum(values.reshape(rows // 8, 8, width), axis=0)
    return sum(total[:, start : start + LANES] for start in range(0, width, LANES))


def mean_part(own, smooth, arrived, mean, change):
    log_mean = own[...] + arrived[...]
    values = jnp.exp(log_mean)
    mean[...] = values
    change[...] = log_mean - smooth[...]
    return folded(values)


def inner_mean_kernel(own, smooth, arrived, mean, change, partial):
    partial[...] = mean_part(own, smooth, arrived, mean, change)


def rim_mean_kernel(own, smooth, arrived, inner_own, before, mean, change, partial, later):
    partial[...] = before[...] + mean_part(own, smooth, arrived, mean, change)
    rest = later.shape[0] - HALF
    later[:HALF, :] = own[:HALF, :]
    later[HALF:rest, :] = inner_own[...]
    later[rest:, :] = own[HALF:, :]


def later_mean_kernel(rim_own, rim_smooth, inner_own, inner_smooth, later, mean, change):
    rest = mean.shape[0] - HALF
    for rows, own, smooth in (
        (slice(0, HALF), rim_own[:HALF, :], rim_smooth[:HALF, :]),
        (slice(HALF, rest), inner_own[...], inner_smooth[...]),
        (slice(rest, rest + HALF), rim_own[HALF:, :], rim_smooth[HALF:, :]),
    ):
        log_mean = own + later[rows, :]
        mean[rows, :] = jnp.exp(log_mean)
        change[rows, :] = log_mean - smooth


def final_kernel(
    cells, total, rim_mean, rim_change, inner_mean, inner_change, later_mean, later_change, barycenter, new_logs,
    stage, sems,
):
    height, width = barycenter.shape
    share = width // 2
    scale = cells / jnp.sum(total[...], axis=(0, 1), keepdims=True)
    log_scale = jnp.log(scale)
    copies = []
    for k, (out, rim, inner, later, apply) in enumerate(
        (
            (barycenter, rim_mean, inner_mean, later_mean, lambda x: x * scale),
            (new_logs, rim_change, inner_change, later_change, lambda x: x + log_scale),
        )
    ):
        for step, which in enumerate(("own", "other")):
            slot = slice(step * share, (step + 1) * share)
            if which == "own":
                stage[k, :HALF, slot] = apply(rim[:HALF, :])
                stage[k, HALF : height - HALF, slot] = apply(inner[...])
                stage[k, height - HALF :, slot] = apply(rim[HALF:, :])
            else:
                stage[k, :, slot] = apply(later[...])
            lanes = pl.ds(pl.multiple_of(half_place(which) * share, LANES), share)
            copy = pltpu.make_async_copy(stage.at[k, :, slot], out.at[:, lanes], sems.at[k, step])
            copy.start()
            copies.append(copy)
    for copy in copies:
        copy.wait()


def call(kernel, name, args, outs, scratch=(), cost=0, far_out=False, sems=None):
    shaped = lambda shape: shape if isinstance(shape, jax.ShapeDtypeStruct) else jax.ShapeDtypeStruct(shape, jnp.float32)
    near = pl.BlockSpec(memory_space=pltpu.VMEM)
    far = pl.BlockSpec(memory_space=pl.ANY)
    return pl.pallas_call(
        kernel,
        name=name,
        out_shape=tuple(shaped(shape) for shape in outs),
        in_specs=[near for _ in args],
        out_specs=tuple(far if far_out else near for _ in outs),
        scratch_shapes=[pltpu.VMEM(shape, jnp.float32) for shape in scratch]
        + ([pltpu.SemaphoreType.DMA(sems)] if sems else []),
        compiler_params=pltpu.CompilerParams(vmem_limit_bytes=32 * 1024 * 1024),
        cost_estimate=pl.CostEstimate(flops=5 * cost, bytes_accessed=cost // 256, transcendentals=0),
    )(*args)


def swap_columns(edges):
    count = lax.axis_size("cols")
    if count == 2:
        got = lax.ppermute(edges[0], "cols", [(0, 1), (1, 0)])
        return got, got
    steps = [(i, i + 1) for i in range(count - 1)]
    right_edge, left_edge = edges
    return (
        lax.ppermute(right_edge, "cols", steps),
        lax.ppermute(left_edge, "cols", [(b, a) for a, b in steps]),
    )


def swap_rows(flip, first, second):
    count = lax.axis_size("rows")
    pairs = lambda start: [
        pair for i in range(start, count - 1, 2) for pair in ((i, i + 1), (i + 1, i))
    ]
    return lax.ppermute(first, "rows", pairs(flip)), lax.ppermute(second, "rows", pairs(1 - flip))


def swap_hist(values):
    return lax.ppermute(values, "hist", [(0, 1), (1, 0)])


def total_over(values, axes):
    count = lax.axis_size(axes)
    if count & (count - 1):
        return lax.psum(values, axes)
    arrived = [lax.ppermute(values, axes, [(i, i ^ mask) for i in range(count)]) for mask in range(1, count)]
    return values + sum(arrived)


def body(hists, log_scaling_fields, histogram_weight_list):
    masses = hists[0]
    logs = log_scaling_fields[0]
    weights = histogram_weight_list
    height, width = masses.shape
    count = lax.axis_size("hist")
    edge = 2 * HALF
    inner = height - edge
    share = width // 2
    wide_width = width + LANES
    matmul = 2 * height * width * 3 * 256
    cells = height * lax.axis_size("rows") * width * lax.axis_size("cols")

    half = lambda *shape: jax.ShapeDtypeStruct(shape, jnp.bfloat16)
    taps, inner_taps, rim_taps = call(
        bands_kernel, "bands", (),
        [half(LANES + edge, 2 * LANES), half(2 * inner, 2 * height), half(edge, 2 * (HALF + edge))],
    )
    flips = {"other": (0, 0), "own": (1, 0)}
    sides = 1 if lax.axis_size("cols") == 2 else 2
    tiles = [(height, LANES)] * sides
    logs, *edges = call(log_edge_kernel, "log_edges", (logs, taps), [(height, width)] + tiles)
    from_left, from_right = swap_columns(edges)
    (partial,) = call(
        spread_kernel, "spread", (logs, taps), [(height, wide_width)], [(height, wide_width)], cost=matmul
    )
    across, *other_sent = call(
        spread_edge_kernel, "spread_edge", (partial, logs, from_left, from_right, taps),
        [(height, wide_width)] + [(HALF, share + LANES)] * 2, cost=matmul // 8,
    )
    first, second, *edges = call(
        mass_edge_kernel, "mass_edges", (masses, across, other_sent[0]), [(HALF, share + LANES)] * 2 + tiles,
        cost=20 * matmul,
    )
    own_sent = (first, second)
    from_left, from_right = swap_columns(edges)
    other_arrived = swap_rows(0, *other_sent)
    own_arrived = swap_rows(1, *own_sent)
    inside, masses, weight = call(
        inner_ratio_kernel, "inner_ratio",
        (across, masses, from_left, from_right, weights.reshape(1, count), taps, inner_taps),
        [(inner, width), (height, wide_width), (8, LANES)], [(inner, wide_width), (inner, wide_width)],
    )

    def rim_ratio(which, arrived, after):
        return call(
            functools.partial(rim_ratio_kernel, which, flips[which][0]), which + "_rim_ratio",
            (across, *arrived, masses, taps, rim_taps, after),
            [(edge, share)], [(edge, share + LANES)] * 2, cost=matmul,
        )[0]

    def inner_log(which, rims):
        return call(
            functools.partial(inner_log_kernel, which), which + "_inner_log",
            (weight, rims, inside, logs, inner_taps), [(inner, share)] * 2, cost=matmul,
        )

    def rim_log(which, rims, arrived, after):
        return call(
            functools.partial(rim_log_kernel, which, flips[which][1]), which + "_rim_log",
            (weight, *arrived, rims, inside, logs, rim_taps, after), [(edge, share)] * 2, cost=matmul,
        )

    def rim_exchange(which, rims, after):
        goes = flips[which][1]
        sent = call(
            functools.partial(rim_sends_kernel, goes), which + "_rim_sends", (rims, after), [(HALF, share)] * 2,
            cost=0 * matmul,
        )
        return swap_rows(goes, *sent)

    other_rims = rim_ratio("other", other_arrived, inside)
    other_inner_smooth, other_inner_own = inner_log("other", other_rims)
    other_arrived = rim_exchange("other", other_rims, other_inner_own)
    own_rims = rim_ratio("own", own_arrived, other_inner_own)
    inner_smooth, inner_own = inner_log("own", own_rims)
    own_arrived = rim_exchange("own", own_rims, inner_own)
    other_rim_smooth, other_rim_own = rim_log("other", other_rims, other_arrived, inner_own)
    rim_smooth, rim_own = rim_log("own", own_rims, own_arrived, other_rim_own)

    if count != 2:
        joined = lambda rim, inside: jnp.concatenate([rim[:HALF], inside, rim[HALF:]], axis=0)
        both = lambda *parts: jnp.concatenate([joined(*parts[:2]), joined(*parts[2:])], axis=1)
        log_mean = lax.psum(both(rim_own, inner_own, other_rim_own, other_inner_own), "hist")
        log_smooth = both(rim_smooth, inner_smooth, other_rim_smooth, other_inner_smooth)
        mean = jnp.exp(log_mean)
        scale = cells / lax.psum(jnp.sum(mean), ("rows", "cols"))
        return (mean * scale, (log_mean + jnp.log(scale) - log_smooth)[None])

    inner_arrived = swap_hist(other_inner_own)
    rim_arrived = swap_hist(other_rim_own)
    inner_mean, inner_change, mass = call(
        inner_mean_kernel, "inner_mean", (inner_own, inner_smooth, inner_arrived),
        [(inner, share), (inner, share), (8, LANES)], cost=matmul // 4,
    )
    rim_mean, rim_change, mass, later = call(
        rim_mean_kernel, "rim_mean", (rim_own, rim_smooth, rim_arrived, inner_own, mass),
        [(edge, share), (edge, share), (8, LANES), (height, share)], cost=matmul // 4,
    )
    later_arrived = swap_hist(later)
    mass = total_over(mass, ("rows",))
    mass = total_over(mass, ("hist", "cols"))
    later_mean, later_change = call(
        later_mean_kernel, "later_mean",
        (other_rim_own, other_rim_smooth, other_inner_own, other_inner_smooth, later_arrived),
        [(height, share)] * 2, cost=matmul // 4,
    )
    barycenter, new_logs = call(
        functools.partial(final_kernel, float(cells)), "final",
        (mass, rim_mean, rim_change, inner_mean, inner_change, later_mean, later_change),
        [(height, width)] * 2, [(2, height, width)], far_out=True, sems=(2, 2), cost=matmul // 4,
    )
    return (barycenter, new_logs[None])


def solution(mesh):
    return jax.shard_map(
        body,
        mesh=mesh,
        in_specs=(
            P("hist", ("groups", "rows"), "cols"),
            P("hist", ("groups", "rows"), "cols"),
            P(),
        ),
        out_specs=(P(("groups", "rows"), "cols"), P("hist", ("groups", "rows"), "cols")),
        check_vma=False,
    )
```

```python
import functools

import jax
import jax.numpy as jnp
import numpy as np
from jax import lax
from jax.experimental import pallas as pl
from jax.experimental.pallas import tpu as pltpu
from jax.sharding import PartitionSpec as P

HALF = 32
LANES = 128
kernel_sigma = 16.0


def taps_total():
    taps = np.arange(-HALF, HALF + 1).astype(np.float64)
    return float(np.sum(np.exp(-taps * taps / (2.0 * kernel_sigma * kernel_sigma))))


def band_matrix(shape, axis_in):
    places = lax.broadcasted_iota(jnp.int32, shape, axis_in) - lax.broadcasted_iota(jnp.int32, shape, 1 - axis_in)
    offsets = (places - HALF).astype(jnp.float32)
    entries = jnp.exp(-offsets * offsets / (2.0 * kernel_sigma * kernel_sigma)) / taps_total()
    return jnp.where(jnp.abs(offsets) <= HALF, entries, 0.0)


def bands_kernel(columns, inner, rim):
    high, low = split(band_matrix((LANES + 2 * HALF, LANES), 0))
    columns[...] = jnp.concatenate([high, low], axis=1)
    for rows in (inner, rim):
        count = rows.shape[0] // 2
        high, low = split(band_matrix((count, count + 2 * HALF), 1))
        rows[...] = jnp.concatenate(
            [jnp.concatenate([high, high], axis=1), jnp.concatenate([low, jnp.zeros_like(low)], axis=1)], axis=0
        )


def split(values):
    high = values.astype(jnp.bfloat16)
    low = (values - high.astype(jnp.float32)).astype(jnp.bfloat16)
    return high, low


def dot(left, right):
    return jnp.dot(left, right, preferred_element_type=jnp.float32)


def column_block(window, band):
    high, low = split(window)
    depth = window.shape[1]
    both = dot(high, band[:depth])
    return both[:, :LANES] + both[:, LANES:] + dot(low, band[:depth, :LANES])


def row_block(window, band):
    high, low = split(window)
    rows = band.shape[0] // 2
    both = dot(band, jnp.concatenate([high, low], axis=0))
    return both[:rows] + both[rows:]


def edge_flags():
    place = lax.axis_index("cols")
    return (place > 0).astype(jnp.float32), (place < lax.axis_size("cols") - 1).astype(jnp.float32)


def row_parity(flip):
    return lax.rem(lax.axis_index("rows") + flip, 2)


def chunks(width, step):
    return [(start, min(start + step, width)) for start in range(0, width, step)]


def edge_sides():
    return [lax.axis_index("cols") == 0] if lax.axis_size("cols") == 2 else [True, False]


def edge_tiles(values, outs):
    width = values.shape[1]
    for out, right in zip(outs, edge_sides()):
        start = pl.multiple_of(jnp.where(right, width - LANES, 0), LANES)
        out[...] = values[:, pl.ds(start, LANES)]


def log_edge_kernel(logs, taps, kept, *outs):
    edge_tiles(logs, outs)
    for out in outs:
        out[...] = jnp.exp(out[...])
    kept[...] = logs[...]


def half_sends(which, flip, across, first, second):
    height, share = across.shape[0], first.shape[1] - LANES
    odd = row_parity(flip)
    lanes = pl.ds(pl.multiple_of(half_place(which) * share, LANES), share + LANES)
    first[...] = across[pl.ds(pl.multiple_of((1 - odd) * (height - HALF), HALF), HALF), lanes]
    second[...] = across[pl.ds(pl.multiple_of(odd * (height - HALF), HALF), HALF), lanes]


def mass_edge_kernel(masses, across, after, first, second, *outs):
    half_sends("own", 1, across, first, second)
    edge_tiles(masses, outs)


def spread_kernel(logs, taps, across, wide):
    width = logs.shape[1]
    edge = 2 * HALF
    wide[:, edge : edge + width] = jnp.exp(logs[...])
    for start in range(LANES, width, LANES):
        across[:, start : start + LANES] = column_block(wide[:, start : start + LANES + 2 * HALF], taps[...])


def spread_edge_kernel(partial, logs, from_left, from_right, taps, across, first, second):
    has_left, has_right = edge_flags()
    height, width = logs.shape
    edge = 2 * HALF
    left = jnp.concatenate([from_left[:, edge:] * has_left, jnp.exp(logs[:, :LANES])], axis=1)
    right = jnp.concatenate([jnp.exp(logs[:, width - edge :]), from_right[:, :edge] * has_right], axis=1)
    across[:, :LANES] = column_block(left, taps[...])
    across[:, width : width + LANES] = column_block(right, taps[...])
    half_sends("other", 0, across, first, second)


def ratio_of(masses, smooth):
    return jnp.where(masses > 0.0, masses / smooth, 0.0)


def column_pass(ratios, taps, out):
    for start in range(0, out.shape[1], LANES):
        out[:, start : start + LANES] = column_block(ratios[:, start : start + LANES + 2 * HALF], taps[...])


def own_weight(weights):
    mine = lax.broadcasted_iota(jnp.int32, weights.shape, 1) == lax.axis_index("hist")
    own = jnp.sum(jnp.where(mine, weights[...], 0.0), axis=1, keepdims=True)
    return own / jnp.sum(weights[...], axis=1, keepdims=True)


def inner_ratio_kernel(
    across, masses, from_left, from_right, weights, taps, row_taps, out, wide, weight, smooth, ratios
):
    weight[...] = jnp.broadcast_to(own_weight(weights), weight.shape)
    has_left, has_right = edge_flags()
    height = masses.shape[0]
    wide[...] = jnp.concatenate(
        [
            from_left[:, LANES - HALF :] * has_left,
            masses[...],
            from_right[:, :HALF] * has_right,
            jnp.zeros((height, 2 * HALF), jnp.float32),
        ],
        axis=1,
    )
    for start, stop in chunks(across.shape[1], 256):
        smooth[:, start:stop] = row_block(across[:, start:stop], row_taps[...])
    ratios[...] = ratio_of(wide[HALF : height - HALF, :], smooth[...])
    column_pass(ratios, taps, out)


def half_place(which):
    place = lax.axis_index("hist") if lax.axis_size("hist") == 2 else 0
    return 1 - place if which == "other" else place


def rim_ratio_kernel(
    which, came, across, first, second, wide, taps, row_taps, after, rims, smooth, ratios
):
    height = across.shape[0]
    share = rims.shape[1]
    odd = row_parity(came)
    offset = half_place(which) * share
    for start, stop in chunks(share + LANES, 256):
        lanes = pl.ds(pl.multiple_of(offset + start, LANES), stop - start)
        one, two = first[:, start:stop], second[:, start:stop]
        upper = jnp.concatenate([jnp.where(odd == 1, one, two), across[: 2 * HALF, lanes]], axis=0)
        lower = jnp.concatenate([across[height - 2 * HALF :, lanes], jnp.where(odd == 1, two, one)], axis=0)
        smooth[:HALF, start:stop] = row_block(upper, row_taps[...])
        smooth[HALF:, start:stop] = row_block(lower, row_taps[...])
    lanes = pl.ds(pl.multiple_of(offset, LANES), share + LANES)
    masses = jnp.concatenate([wide[:HALF, lanes], wide[height - HALF :, lanes]], axis=0)
    ratios[...] = ratio_of(masses, smooth[...])
    column_pass(ratios, taps, rims)


def inner_log_kernel(which, weight, rims, inner, logs, row_taps, smooth, own):
    height = logs.shape[0]
    share = rims.shape[1]
    offset = half_place(which) * share
    for start, stop in chunks(share, 256):
        lanes = pl.ds(pl.multiple_of(offset + start, LANES), stop - start)
        window = jnp.concatenate([rims[:HALF, start:stop], inner[:, lanes], rims[HALF:, start:stop]], axis=0)
        smooth[:, start:stop] = jnp.log(row_block(window, row_taps[...]))
    lanes = pl.ds(pl.multiple_of(offset, LANES), share)
    own[...] = weight[:1, :1] * (logs[HALF : height - HALF, lanes] + smooth[...])


def rim_sends_kernel(goes, rims, after, sent_first, sent_second):
    odd = row_parity(goes)
    sent_first[...] = rims[pl.ds(pl.multiple_of((1 - odd) * HALF, HALF), HALF), :]
    sent_second[...] = rims[pl.ds(pl.multiple_of(odd * HALF, HALF), HALF), :]


def rim_log_kernel(which, came, weight, from_first, from_second, rims, inner, logs, row_taps, after, smooth, own):
    height = logs.shape[0]
    depth = inner.shape[0]
    share = rims.shape[1]
    odd = row_parity(came)
    offset = half_place(which) * share
    for start, stop in chunks(share, 256):
        lanes = pl.ds(pl.multiple_of(offset + start, LANES), stop - start)
        one, two = from_first[:, start:stop], from_second[:, start:stop]
        above, below = jnp.where(odd == 1, one, two), jnp.where(odd == 1, two, one)
        upper = jnp.concatenate([above, rims[:HALF, start:stop], inner[:HALF, lanes]], axis=0)
        lower = jnp.concatenate([inner[depth - HALF :, lanes], rims[HALF:, start:stop], below], axis=0)
        smooth[:HALF, start:stop] = jnp.log(row_block(upper, row_taps[...]))
        smooth[HALF:, start:stop] = jnp.log(row_block(lower, row_taps[...]))
    lanes = pl.ds(pl.multiple_of(offset, LANES), share)
    log_rows = jnp.concatenate([logs[:HALF, lanes], logs[height - HALF :, lanes]], axis=0)
    own[...] = weight[:1, :1] * (log_rows + smooth[...])


def folded(values):
    rows, width = values.shape
    total = jnp.sum(values.reshape(rows // 8, 8, width), axis=0)
    return sum(total[:, start : start + LANES] for start in range(0, width, LANES))


def mean_part(own, smooth, arrived, mean, change):
    log_mean = own[...] + arrived[...]
    values = jnp.exp(log_mean)
    mean[...] = values
    change[...] = log_mean - smooth[...]
    return folded(values)


def inner_mean_kernel(own, smooth, arrived, after, mean, change, partial):
    partial[...] = mean_part(own, smooth, arrived, mean, change)


def later_kernel(rim_own, inner_own, after, later):
    rest = later.shape[0] - HALF
    later[:HALF, :] = rim_own[:HALF, :]
    later[HALF:rest, :] = inner_own[...]
    later[rest:, :] = rim_own[HALF:, :]


def rim_mean_kernel(own, smooth, arrived, before, mean, change, partial):
    partial[...] = before[...] + mean_part(own, smooth, arrived, mean, change)


def later_mean_kernel(rim_own, rim_smooth, inner_own, inner_smooth, later, mean, change):
    rest = mean.shape[0] - HALF
    for rows, own, smooth in (
        (slice(0, HALF), rim_own[:HALF, :], rim_smooth[:HALF, :]),
        (slice(HALF, rest), inner_own[...], inner_smooth[...]),
        (slice(rest, rest + HALF), rim_own[HALF:, :], rim_smooth[HALF:, :]),
    ):
        log_mean = own + later[rows, :]
        mean[rows, :] = jnp.exp(log_mean)
        change[rows, :] = log_mean - smooth


def final_kernel(
    cells, total, rim_mean, rim_change, inner_mean, inner_change, later_mean, later_change, barycenter, new_logs,
    stage, sems,
):
    height, width = barycenter.shape
    share = width // 2
    scale = cells / jnp.sum(total[...], axis=(0, 1), keepdims=True)
    log_scale = jnp.log(scale)
    copies = []
    for k, (out, rim, inner, later, apply) in enumerate(
        (
            (barycenter, rim_mean, inner_mean, later_mean, lambda x: x * scale),
            (new_logs, rim_change, inner_change, later_change, lambda x: x + log_scale),
        )
    ):
        for step, which in enumerate(("own", "other")):
            slot = slice(step * share, (step + 1) * share)
            if which == "own":
                stage[k, :HALF, slot] = apply(rim[:HALF, :])
                stage[k, HALF : height - HALF, slot] = apply(inner[...])
                stage[k, height - HALF :, slot] = apply(rim[HALF:, :])
            else:
                stage[k, :, slot] = apply(later[...])
            lanes = pl.ds(pl.multiple_of(half_place(which) * share, LANES), share)
            copy = pltpu.make_async_copy(stage.at[k, :, slot], out.at[:, lanes], sems.at[k, step])
            copy.start()
            copies.append(copy)
    for copy in copies:
        copy.wait()


def call(kernel, name, args, outs, scratch=(), cost=0, aliases={}, far_out=False, sems=None):
    shaped = lambda shape: shape if isinstance(shape, jax.ShapeDtypeStruct) else jax.ShapeDtypeStruct(shape, jnp.float32)
    near = pl.BlockSpec(memory_space=pltpu.VMEM)
    far = pl.BlockSpec(memory_space=pl.ANY)
    return pl.pallas_call(
        kernel,
        name=name,
        input_output_aliases=aliases,
        out_shape=tuple(shaped(shape) for shape in outs),
        in_specs=[near for _ in args],
        out_specs=tuple(far if far_out else near for _ in outs),
        scratch_shapes=[pltpu.VMEM(shape, jnp.float32) for shape in scratch]
        + ([pltpu.SemaphoreType.DMA(sems)] if sems else []),
        compiler_params=pltpu.CompilerParams(vmem_limit_bytes=32 * 1024 * 1024),
        cost_estimate=pl.CostEstimate(flops=5 * cost, bytes_accessed=cost // 256, transcendentals=0),
    )(*args)


def swap_columns(edges):
    count = lax.axis_size("cols")
    if count == 2:
        got = lax.ppermute(edges[0], "cols", [(0, 1), (1, 0)])
        return got, got
    steps = [(i, i + 1) for i in range(count - 1)]
    right_edge, left_edge = edges
    return (
        lax.ppermute(right_edge, "cols", steps),
        lax.ppermute(left_edge, "cols", [(b, a) for a, b in steps]),
    )


def swap_rows(flip, first, second):
    count = lax.axis_size("rows")
    pairs = lambda start: [
        pair for i in range(start, count - 1, 2) for pair in ((i, i + 1), (i + 1, i))
    ]
    return lax.ppermute(first, "rows", pairs(flip)), lax.ppermute(second, "rows", pairs(1 - flip))


def swap_hist(values):
    return lax.ppermute(values, "hist", [(0, 1), (1, 0)])


def total_over(values, axes):
    count = lax.axis_size(axes)
    if count & (count - 1):
        return lax.psum(values, axes)
    arrived = [lax.ppermute(values, axes, [(i, i ^ mask) for i in range(count)]) for mask in range(1, count)]
    return values + sum(arrived)


def apart(index, mask, span):
    return (index // span ^ mask // span) * span + (index % span ^ mask % span)


def total_aside(values):
    hist, rows, cols = (lax.axis_size(axis) for axis in ("hist", "rows", "cols"))
    if hist & (hist - 1) or cols & (cols - 1):
        return lax.psum(values, ("hist", "cols"))
    aside = cols if rows % 2 == 0 else 0
    total = values
    for k in range(hist):
        for m in range(cols):
            if k or m:
                mask = k * rows * cols + (aside if k else 0) + m
                total = total + lax.ppermute(
                    values, ("hist", "rows", "cols"), [(i, apart(i, mask, rows * cols)) for i in range(hist * rows * cols)]
                )
    return total


def body(hists, log_scaling_fields, histogram_weight_list):
    masses = hists[0]
    logs = log_scaling_fields[0]
    weights = histogram_weight_list
    height, width = masses.shape
    count = lax.axis_size("hist")
    edge = 2 * HALF
    inner = height - edge
    share = width // 2
    wide_width = width + LANES
    matmul = 2 * height * width * 3 * 256
    cells = height * lax.axis_size("rows") * width * lax.axis_size("cols")

    half = lambda *shape: jax.ShapeDtypeStruct(shape, jnp.bfloat16)
    taps, inner_taps, rim_taps = call(
        bands_kernel, "bands", (),
        [half(LANES + edge, 2 * LANES), half(2 * inner, 2 * height), half(edge, 2 * (HALF + edge))],
    )
    flips = {"other": (0, 0), "own": (1, 0)}
    sides = 1 if lax.axis_size("cols") == 2 else 2
    tiles = [(height, LANES)] * sides
    logs, *edges = call(log_edge_kernel, "log_edges", (logs, taps), [(height, width)] + tiles)
    from_left, from_right = swap_columns(edges)
    (partial,) = call(
        spread_kernel, "spread", (logs, taps), [(height, wide_width)], [(height, wide_width)], cost=matmul
    )
    across, *other_sent = call(
        spread_edge_kernel, "spread_edge", (partial, logs, from_left, from_right, taps),
        [(height, wide_width)] + [(HALF, share + LANES)] * 2, cost=matmul // 8, aliases={0: 0},
    )
    first, second, *edges = call(
        mass_edge_kernel, "mass_edges", (masses, across, other_sent[0]), [(HALF, share + LANES)] * 2 + tiles,
        cost=20 * matmul,
    )
    own_sent = (first, second)
    from_left, from_right = swap_columns(edges)
    other_arrived = swap_rows(0, *other_sent)
    own_arrived = swap_rows(1, *own_sent)
    inside, masses, weight = call(
        inner_ratio_kernel, "inner_ratio",
        (across, masses, from_left, from_right, weights.reshape(1, count), taps, inner_taps),
        [(inner, width), (height, wide_width), (8, LANES)], [(inner, wide_width), (inner, wide_width)],
    )

    def rim_ratio(which, arrived, after):
        return call(
            functools.partial(rim_ratio_kernel, which, flips[which][0]), which + "_rim_ratio",
            (across, *arrived, masses, taps, rim_taps, after),
            [(edge, share)], [(edge, share + LANES)] * 2, cost=matmul,
        )[0]

    def inner_log(which, rims):
        return call(
            functools.partial(inner_log_kernel, which), which + "_inner_log",
            (weight, rims, inside, logs, inner_taps), [(inner, share)] * 2, cost=matmul,
        )

    def rim_log(which, rims, arrived, after):
        return call(
            functools.partial(rim_log_kernel, which, flips[which][1]), which + "_rim_log",
            (weight, *arrived, rims, inside, logs, rim_taps, after), [(edge, share)] * 2, cost=matmul,
        )

    def rim_exchange(which, rims, after):
        goes = flips[which][1]
        sent = call(
            functools.partial(rim_sends_kernel, goes), which + "_rim_sends", (rims, after), [(HALF, share)] * 2,
            cost=0 * matmul,
        )
        return swap_rows(goes, *sent)

    other_rims = rim_ratio("other", other_arrived, inside)
    other_inner_smooth, other_inner_own = inner_log("other", other_rims)
    other_arrived = rim_exchange("other", other_rims, other_inner_own)
    own_rims = rim_ratio("own", own_arrived, other_inner_own)
    inner_smooth, inner_own = inner_log("own", own_rims)
    own_arrived = rim_exchange("own", own_rims, inner_own)
    other_rim_smooth, other_rim_own = rim_log("other", other_rims, other_arrived, inner_own)
    rim_smooth, rim_own = rim_log("own", own_rims, own_arrived, other_rim_own)

    if count != 2:
        joined = lambda rim, inside: jnp.concatenate([rim[:HALF], inside, rim[HALF:]], axis=0)
        both = lambda *parts: jnp.concatenate([joined(*parts[:2]), joined(*parts[2:])], axis=1)
        log_mean = lax.psum(both(rim_own, inner_own, other_rim_own, other_inner_own), "hist")
        log_smooth = both(rim_smooth, inner_smooth, other_rim_smooth, other_inner_smooth)
        mean = jnp.exp(log_mean)
        scale = cells / lax.psum(jnp.sum(mean), ("rows", "cols"))
        return (mean * scale, (log_mean + jnp.log(scale) - log_smooth)[None])

    inner_arrived = swap_hist(other_inner_own)
    rim_arrived = swap_hist(other_rim_own)
    inner_mean, inner_change, mass = call(
        inner_mean_kernel, "inner_mean", (inner_own, inner_smooth, inner_arrived, rim_own),
        [(inner, share), (inner, share), (8, LANES)], cost=matmul // 4,
    )
    turn = lax.ppermute(mass, "cols", [(i, i ^ 1) for i in range(lax.axis_size("cols") // 2 * 2)])
    (later,) = call(later_kernel, "later", (rim_own, inner_own, turn), [(height, share)], cost=matmul // 4)
    rim_mean, rim_change, mass = call(
        rim_mean_kernel, "rim_mean", (rim_own, rim_smooth, rim_arrived, mass),
        [(edge, share), (edge, share), (8, LANES)], cost=10 * matmul,
    )
    later_arrived = swap_hist(later)
    mass = total_over(mass, ("rows",))
    mass = total_aside(mass)
    later_mean, later_change = call(
        later_mean_kernel, "later_mean",
        (other_rim_own, other_rim_smooth, other_inner_own, other_inner_smooth, later_arrived),
        [(height, share)] * 2, cost=matmul // 4,
    )
    barycenter, new_logs = call(
        functools.partial(final_kernel, float(cells)), "final",
        (mass, rim_mean, rim_change, inner_mean, inner_change, later_mean, later_change),
        [(height, width)] * 2, [(2, height, width)], far_out=True, sems=(2, 2), cost=matmul // 4,
    )
    return (barycenter, new_logs[None])


def solution(mesh):
    return jax.shard_map(
        body,
        mesh=mesh,
        in_specs=(
            P("hist", ("groups", "rows"), "cols"),
            P("hist", ("groups", "rows"), "cols"),
            P(),
        ),
        out_specs=(P(("groups", "rows"), "cols"), P("hist", ("groups", "rows"), "cols")),
        check_vma=False,
    )
```

```python
import functools

import jax
import jax.numpy as jnp
import numpy as np
from jax import lax
from jax.experimental import pallas as pl
from jax.experimental.pallas import tpu as pltpu
from jax.sharding import PartitionSpec as P

HALF = 32
LANES = 128
kernel_sigma = 16.0


def taps_total():
    taps = np.arange(-HALF, HALF + 1).astype(np.float64)
    return float(np.sum(np.exp(-taps * taps / (2.0 * kernel_sigma * kernel_sigma))))


def band_matrix(shape, axis_in):
    places = lax.broadcasted_iota(jnp.int32, shape, axis_in) - lax.broadcasted_iota(jnp.int32, shape, 1 - axis_in)
    offsets = (places - HALF).astype(jnp.float32)
    entries = jnp.exp(-offsets * offsets / (2.0 * kernel_sigma * kernel_sigma)) / taps_total()
    return jnp.where(jnp.abs(offsets) <= HALF, entries, 0.0)


def bands_kernel(columns, inner, rim):
    high, low = split(band_matrix((LANES + 2 * HALF, LANES), 0))
    columns[...] = jnp.concatenate([high, low], axis=1)
    for rows in (inner, rim):
        count = rows.shape[0] // 2
        high, low = split(band_matrix((count, count + 2 * HALF), 1))
        rows[...] = jnp.concatenate(
            [jnp.concatenate([high, high], axis=1), jnp.concatenate([low, jnp.zeros_like(low)], axis=1)], axis=0
        )


def split(values):
    high = values.astype(jnp.bfloat16)
    low = (values - high.astype(jnp.float32)).astype(jnp.bfloat16)
    return high, low


def dot(left, right):
    return jnp.dot(left, right, preferred_element_type=jnp.float32)


def column_block(window, band):
    high, low = split(window)
    depth = window.shape[1]
    both = dot(high, band[:depth])
    return both[:, :LANES] + both[:, LANES:] + dot(low, band[:depth, :LANES])


def row_block(window, band):
    high, low = split(window)
    rows = band.shape[0] // 2
    both = dot(band, jnp.concatenate([high, low], axis=0))
    return both[:rows] + both[rows:]


def edge_flags():
    place = lax.axis_index("cols")
    return (place > 0).astype(jnp.float32), (place < lax.axis_size("cols") - 1).astype(jnp.float32)


def row_parity(flip):
    return lax.rem(lax.axis_index("rows") + flip, 2)


def chunks(width, step):
    return [(start, min(start + step, width)) for start in range(0, width, step)]


def edge_sides():
    return [lax.axis_index("cols") == 0] if lax.axis_size("cols") == 2 else [True, False]


def edge_tiles(values, outs):
    width = values.shape[1]
    for out, right in zip(outs, edge_sides()):
        start = pl.multiple_of(jnp.where(right, width - LANES, 0), LANES)
        out[...] = values[:, pl.ds(start, LANES)]


def log_edge_kernel(logs, taps, kept, *outs):
    edge_tiles(logs, outs)
    for out in outs:
        out[...] = jnp.exp(out[...])
    kept[...] = logs[...]


def half_sends(which, flip, across, first, second):
    height, share = across.shape[0], first.shape[1] - LANES
    odd = row_parity(flip)
    lanes = pl.ds(pl.multiple_of(half_place(which) * share, LANES), share + LANES)
    first[...] = across[pl.ds(pl.multiple_of((1 - odd) * (height - HALF), HALF), HALF), lanes]
    second[...] = across[pl.ds(pl.multiple_of(odd * (height - HALF), HALF), HALF), lanes]


def mass_edge_kernel(masses, across, after, first, second, *outs):
    half_sends("own", 1, across, first, second)
    edge_tiles(masses, outs)


def spread_kernel(logs, taps, across, wide):
    width = logs.shape[1]
    edge = 2 * HALF
    wide[:, edge : edge + width] = jnp.exp(logs[...])
    for start in range(LANES, width, LANES):
        across[:, start : start + LANES] = column_block(wide[:, start : start + LANES + 2 * HALF], taps[...])


def spread_edge_kernel(partial, logs, from_left, from_right, taps, across, first, second):
    has_left, has_right = edge_flags()
    height, width = logs.shape
    edge = 2 * HALF
    left = jnp.concatenate([from_left[:, edge:] * has_left, jnp.exp(logs[:, :LANES])], axis=1)
    right = jnp.concatenate([jnp.exp(logs[:, width - edge :]), from_right[:, :edge] * has_right], axis=1)
    across[:, :LANES] = column_block(left, taps[...])
    across[:, width : width + LANES] = column_block(right, taps[...])
    half_sends("other", 0, across, first, second)


def ratio_of(masses, smooth):
    return jnp.where(masses > 0.0, masses / smooth, 0.0)


def column_pass(ratios, taps, out):
    for start in range(0, out.shape[1], LANES):
        out[:, start : start + LANES] = column_block(ratios[:, start : start + LANES + 2 * HALF], taps[...])


def own_weight(weights):
    mine = lax.broadcasted_iota(jnp.int32, weights.shape, 1) == lax.axis_index("hist")
    own = jnp.sum(jnp.where(mine, weights[...], 0.0), axis=1, keepdims=True)
    return own / jnp.sum(weights[...], axis=1, keepdims=True)


def inner_ratio_kernel(
    across, masses, from_left, from_right, weights, taps, row_taps, out, wide, weight, smooth, ratios
):
    weight[...] = jnp.broadcast_to(own_weight(weights), weight.shape)
    has_left, has_right = edge_flags()
    height = masses.shape[0]
    wide[...] = jnp.concatenate(
        [
            from_left[:, LANES - HALF :] * has_left,
            masses[...],
            from_right[:, :HALF] * has_right,
            jnp.zeros((height, 2 * HALF), jnp.float32),
        ],
        axis=1,
    )
    for start, stop in chunks(across.shape[1], 256):
        smooth[:, start:stop] = row_block(across[:, start:stop], row_taps[...])
    ratios[...] = ratio_of(wide[HALF : height - HALF, :], smooth[...])
    column_pass(ratios, taps, out)


def half_place(which):
    place = lax.axis_index("hist") if lax.axis_size("hist") == 2 else 0
    return 1 - place if which == "other" else place


def rim_ratio_kernel(
    which, came, across, first, second, wide, taps, row_taps, after, rims, smooth, ratios
):
    height = across.shape[0]
    share = rims.shape[1]
    odd = row_parity(came)
    offset = half_place(which) * share
    for start, stop in chunks(share + LANES, 256):
        lanes = pl.ds(pl.multiple_of(offset + start, LANES), stop - start)
        one, two = first[:, start:stop], second[:, start:stop]
        upper = jnp.concatenate([jnp.where(odd == 1, one, two), across[: 2 * HALF, lanes]], axis=0)
        lower = jnp.concatenate([across[height - 2 * HALF :, lanes], jnp.where(odd == 1, two, one)], axis=0)
        smooth[:HALF, start:stop] = row_block(upper, row_taps[...])
        smooth[HALF:, start:stop] = row_block(lower, row_taps[...])
    lanes = pl.ds(pl.multiple_of(offset, LANES), share + LANES)
    masses = jnp.concatenate([wide[:HALF, lanes], wide[height - HALF :, lanes]], axis=0)
    ratios[...] = ratio_of(masses, smooth[...])
    column_pass(ratios, taps, rims)


def inner_log_kernel(which, weight, rims, inner, logs, row_taps, smooth, own):
    height = logs.shape[0]
    share = rims.shape[1]
    offset = half_place(which) * share
    for start, stop in chunks(share, 256):
        lanes = pl.ds(pl.multiple_of(offset + start, LANES), stop - start)
        window = jnp.concatenate([rims[:HALF, start:stop], inner[:, lanes], rims[HALF:, start:stop]], axis=0)
        smooth[:, start:stop] = jnp.log(row_block(window, row_taps[...]))
    lanes = pl.ds(pl.multiple_of(offset, LANES), share)
    own[...] = weight[:1, :1] * (logs[HALF : height - HALF, lanes] + smooth[...])


def rim_sends_kernel(goes, rims, after, sent_first, sent_second):
    odd = row_parity(goes)
    sent_first[...] = rims[pl.ds(pl.multiple_of((1 - odd) * HALF, HALF), HALF), :]
    sent_second[...] = rims[pl.ds(pl.multiple_of(odd * HALF, HALF), HALF), :]


def rim_log_kernel(which, came, weight, from_first, from_second, rims, inner, logs, row_taps, after, smooth, own):
    height = logs.shape[0]
    depth = inner.shape[0]
    share = rims.shape[1]
    odd = row_parity(came)
    offset = half_place(which) * share
    for start, stop in chunks(share, 256):
        lanes = pl.ds(pl.multiple_of(offset + start, LANES), stop - start)
        one, two = from_first[:, start:stop], from_second[:, start:stop]
        above, below = jnp.where(odd == 1, one, two), jnp.where(odd == 1, two, one)
        upper = jnp.concatenate([above, rims[:HALF, start:stop], inner[:HALF, lanes]], axis=0)
        lower = jnp.concatenate([inner[depth - HALF :, lanes], rims[HALF:, start:stop], below], axis=0)
        smooth[:HALF, start:stop] = jnp.log(row_block(upper, row_taps[...]))
        smooth[HALF:, start:stop] = jnp.log(row_block(lower, row_taps[...]))
    lanes = pl.ds(pl.multiple_of(offset, LANES), share)
    log_rows = jnp.concatenate([logs[:HALF, lanes], logs[height - HALF :, lanes]], axis=0)
    own[...] = weight[:1, :1] * (log_rows + smooth[...])


def folded(values):
    rows, width = values.shape
    total = jnp.sum(values.reshape(rows // 8, 8, width), axis=0)
    return sum(total[:, start : start + LANES] for start in range(0, width, LANES))


def mean_part(own, smooth, arrived, mean, change):
    log_mean = own[...] + arrived[...]
    values = jnp.exp(log_mean)
    mean[...] = values
    change[...] = log_mean - smooth[...]
    return folded(values)


def inner_mean_kernel(own, smooth, arrived, after, mean, change, partial):
    partial[...] = mean_part(own, smooth, arrived, mean, change)


def later_kernel(rim_own, inner_own, after, later):
    rest = later.shape[0] - HALF
    later[:HALF, :] = rim_own[:HALF, :]
    later[HALF:rest, :] = inner_own[...]
    later[rest:, :] = rim_own[HALF:, :]


def rim_mean_kernel(own, smooth, arrived, before, mean, change, partial):
    partial[...] = before[...] + mean_part(own, smooth, arrived, mean, change)


def final_kernel(
    cells, total, rim_mean, rim_change, inner_mean, inner_change, rim_own, rim_smooth, inner_own, inner_smooth, later,
    barycenter, new_logs, stage, sems,
):
    height, width = barycenter.shape
    share = width // 2
    rest = height - HALF
    scale = cells / jnp.sum(total[...], axis=(0, 1), keepdims=True)
    log_scale = jnp.log(scale)
    rows = ((slice(0, HALF), slice(0, HALF)), (slice(HALF, rest), slice(None)), (slice(rest, height), slice(HALF, 2 * HALF)))
    copies = []

    def send(k, step, which):
        lanes = pl.ds(pl.multiple_of(half_place(which) * share, LANES), share)
        source = stage.at[k, :, slice(step * share, (step + 1) * share)]
        copy = pltpu.make_async_copy(source, (barycenter, new_logs)[k].at[:, lanes], sems.at[k, step])
        copy.start()
        copies.append(copy)

    for (to, part), mean, change in zip(rows, (rim_mean, inner_mean, rim_mean), (rim_change, inner_change, rim_change)):
        stage[0, to, :share] = mean[part, :] * scale
        stage[1, to, :share] = change[part, :] + log_scale
    send(0, 0, "own")
    send(1, 0, "own")
    for (to, part), own, smooth in zip(rows, (rim_own, inner_own, rim_own), (rim_smooth, inner_smooth, rim_smooth)):
        log_mean = own[part, :] + later[to, :]
        stage[0, to, share:] = jnp.exp(log_mean) * scale
        stage[1, to, share:] = log_mean - smooth[part, :] + log_scale
    send(0, 1, "other")
    send(1, 1, "other")
    for copy in copies:
        copy.wait()


def call(kernel, name, args, outs, scratch=(), cost=0, aliases={}, far_out=False, sems=None):
    shaped = lambda shape: shape if isinstance(shape, jax.ShapeDtypeStruct) else jax.ShapeDtypeStruct(shape, jnp.float32)
    near = pl.BlockSpec(memory_space=pltpu.VMEM)
    far = pl.BlockSpec(memory_space=pl.ANY)
    return pl.pallas_call(
        kernel,
        name=name,
        input_output_aliases=aliases,
        out_shape=tuple(shaped(shape) for shape in outs),
        in_specs=[near for _ in args],
        out_specs=tuple(far if far_out else near for _ in outs),
        scratch_shapes=[pltpu.VMEM(shape, jnp.float32) for shape in scratch]
        + ([pltpu.SemaphoreType.DMA(sems)] if sems else []),
        compiler_params=pltpu.CompilerParams(vmem_limit_bytes=32 * 1024 * 1024),
        cost_estimate=pl.CostEstimate(flops=5 * cost, bytes_accessed=cost // 256, transcendentals=0),
    )(*args)


def swap_columns(edges):
    count = lax.axis_size("cols")
    if count == 2:
        got = lax.ppermute(edges[0], "cols", [(0, 1), (1, 0)])
        return got, got
    steps = [(i, i + 1) for i in range(count - 1)]
    right_edge, left_edge = edges
    return (
        lax.ppermute(right_edge, "cols", steps),
        lax.ppermute(left_edge, "cols", [(b, a) for a, b in steps]),
    )


def swap_rows(flip, first, second):
    count = lax.axis_size("rows")
    pairs = lambda start: [
        pair for i in range(start, count - 1, 2) for pair in ((i, i + 1), (i + 1, i))
    ]
    return lax.ppermute(first, "rows", pairs(flip)), lax.ppermute(second, "rows", pairs(1 - flip))


def swap_hist(values):
    return lax.ppermute(values, "hist", [(0, 1), (1, 0)])


def total_over(values, axes):
    count = lax.axis_size(axes)
    if count & (count - 1):
        return lax.psum(values, axes)
    arrived = [lax.ppermute(values, axes, [(i, i ^ mask) for i in range(count)]) for mask in range(1, count)]
    return values + sum(arrived)


def apart(index, mask, span):
    return (index // span ^ mask // span) * span + (index % span ^ mask % span)


def total_aside(values):
    hist, rows, cols = (lax.axis_size(axis) for axis in ("hist", "rows", "cols"))
    if hist & (hist - 1) or cols & (cols - 1):
        return lax.psum(values, ("hist", "cols"))
    aside = cols if rows % 2 == 0 else 0
    total = values
    for k in range(hist):
        for m in range(cols):
            if k or m:
                mask = k * rows * cols + (aside if k else 0) + m
                total = total + lax.ppermute(
                    values, ("hist", "rows", "cols"), [(i, apart(i, mask, rows * cols)) for i in range(hist * rows * cols)]
                )
    return total


def body(hists, log_scaling_fields, histogram_weight_list):
    masses = hists[0]
    logs = log_scaling_fields[0]
    weights = histogram_weight_list
    height, width = masses.shape
    count = lax.axis_size("hist")
    edge = 2 * HALF
    inner = height - edge
    share = width // 2
    wide_width = width + LANES
    matmul = 2 * height * width * 3 * 256
    cells = height * lax.axis_size("rows") * width * lax.axis_size("cols")

    half = lambda *shape: jax.ShapeDtypeStruct(shape, jnp.bfloat16)
    taps, inner_taps, rim_taps = call(
        bands_kernel, "bands", (),
        [half(LANES + edge, 2 * LANES), half(2 * inner, 2 * height), half(edge, 2 * (HALF + edge))],
    )
    flips = {"other": (0, 0), "own": (1, 0)}
    sides = 1 if lax.axis_size("cols") == 2 else 2
    tiles = [(height, LANES)] * sides
    logs, *edges = call(log_edge_kernel, "log_edges", (logs, taps), [(height, width)] + tiles)
    from_left, from_right = swap_columns(edges)
    (partial,) = call(
        spread_kernel, "spread", (logs, taps), [(height, wide_width)], [(height, wide_width)], cost=matmul
    )
    across, *other_sent = call(
        spread_edge_kernel, "spread_edge", (partial, logs, from_left, from_right, taps),
        [(height, wide_width)] + [(HALF, share + LANES)] * 2, cost=matmul // 8, aliases={0: 0},
    )
    first, second, *edges = call(
        mass_edge_kernel, "mass_edges", (masses, across, other_sent[0]), [(HALF, share + LANES)] * 2 + tiles,
        cost=20 * matmul,
    )
    own_sent = (first, second)
    from_left, from_right = swap_columns(edges)
    other_arrived = swap_rows(0, *other_sent)
    own_arrived = swap_rows(1, *own_sent)
    inside, masses, weight = call(
        inner_ratio_kernel, "inner_ratio",
        (across, masses, from_left, from_right, weights.reshape(1, count), taps, inner_taps),
        [(inner, width), (height, wide_width), (8, LANES)], [(inner, wide_width), (inner, wide_width)],
    )

    def rim_ratio(which, arrived, after):
        return call(
            functools.partial(rim_ratio_kernel, which, flips[which][0]), which + "_rim_ratio",
            (across, *arrived, masses, taps, rim_taps, after),
            [(edge, share)], [(edge, share + LANES)] * 2, cost=matmul,
        )[0]

    def inner_log(which, rims):
        return call(
            functools.partial(inner_log_kernel, which), which + "_inner_log",
            (weight, rims, inside, logs, inner_taps), [(inner, share)] * 2, cost=matmul,
        )

    def rim_log(which, rims, arrived, after):
        return call(
            functools.partial(rim_log_kernel, which, flips[which][1]), which + "_rim_log",
            (weight, *arrived, rims, inside, logs, rim_taps, after), [(edge, share)] * 2, cost=matmul,
        )

    def rim_exchange(which, rims, after):
        goes = flips[which][1]
        sent = call(
            functools.partial(rim_sends_kernel, goes), which + "_rim_sends", (rims, after), [(HALF, share)] * 2,
            cost=0 * matmul,
        )
        return swap_rows(goes, *sent)

    other_rims = rim_ratio("other", other_arrived, inside)
    other_inner_smooth, other_inner_own = inner_log("other", other_rims)
    other_arrived = rim_exchange("other", other_rims, other_inner_own)
    own_rims = rim_ratio("own", own_arrived, other_inner_own)
    inner_smooth, inner_own = inner_log("own", own_rims)
    own_arrived = rim_exchange("own", own_rims, inner_own)
    other_rim_smooth, other_rim_own = rim_log("other", other_rims, other_arrived, inner_own)
    rim_smooth, rim_own = rim_log("own", own_rims, own_arrived, other_rim_own)

    if count != 2:
        joined = lambda rim, inside: jnp.concatenate([rim[:HALF], inside, rim[HALF:]], axis=0)
        both = lambda *parts: jnp.concatenate([joined(*parts[:2]), joined(*parts[2:])], axis=1)
        log_mean = lax.psum(both(rim_own, inner_own, other_rim_own, other_inner_own), "hist")
        log_smooth = both(rim_smooth, inner_smooth, other_rim_smooth, other_inner_smooth)
        mean = jnp.exp(log_mean)
        scale = cells / lax.psum(jnp.sum(mean), ("rows", "cols"))
        return (mean * scale, (log_mean + jnp.log(scale) - log_smooth)[None])

    inner_arrived = swap_hist(other_inner_own)
    rim_arrived = swap_hist(other_rim_own)
    inner_mean, inner_change, mass = call(
        inner_mean_kernel, "inner_mean", (inner_own, inner_smooth, inner_arrived, rim_own),
        [(inner, share), (inner, share), (8, LANES)], cost=matmul // 4,
    )
    turn = lax.ppermute(mass, "cols", [(i, i ^ 1) for i in range(lax.axis_size("cols") // 2 * 2)])
    (later,) = call(later_kernel, "later", (rim_own, inner_own, turn), [(height, share)], cost=matmul // 4)
    rim_mean, rim_change, mass = call(
        rim_mean_kernel, "rim_mean", (rim_own, rim_smooth, rim_arrived, mass),
        [(edge, share), (edge, share), (8, LANES)], cost=10 * matmul,
    )
    later_arrived = swap_hist(later)
    mass = total_over(mass, ("rows",))
    mass = total_aside(mass)
    barycenter, new_logs = call(
        functools.partial(final_kernel, float(cells)), "final",
        (mass, rim_mean, rim_change, inner_mean, inner_change, other_rim_own, other_rim_smooth, other_inner_own,
         other_inner_smooth, later_arrived),
        [(height, width)] * 2, [(2, height, width)], far_out=True, sems=(2, 2), cost=matmul // 4,
    )
    return (barycenter, new_logs[None])


def solution(mesh):
    return jax.shard_map(
        body,
        mesh=mesh,
        in_specs=(
            P("hist", ("groups", "rows"), "cols"),
            P("hist", ("groups", "rows"), "cols"),
            P(),
        ),
        out_specs=(P(("groups", "rows"), "cols"), P("hist", ("groups", "rows"), "cols")),
        check_vma=False,
    )
```

```python
import functools

import jax
import jax.numpy as jnp
import numpy as np
from jax import lax
from jax.experimental import pallas as pl
from jax.experimental.pallas import tpu as pltpu
from jax.sharding import PartitionSpec as P

HALF = 32
LANES = 128
kernel_sigma = 16.0


def taps_total():
    taps = np.arange(-HALF, HALF + 1).astype(np.float64)
    return float(np.sum(np.exp(-taps * taps / (2.0 * kernel_sigma * kernel_sigma))))


def band_matrix(shape, axis_in):
    places = lax.broadcasted_iota(jnp.int32, shape, axis_in) - lax.broadcasted_iota(jnp.int32, shape, 1 - axis_in)
    offsets = (places - HALF).astype(jnp.float32)
    entries = jnp.exp(-offsets * offsets / (2.0 * kernel_sigma * kernel_sigma)) / taps_total()
    return jnp.where(jnp.abs(offsets) <= HALF, entries, 0.0)


def bands_kernel(columns, inner, rim):
    high, low = split(band_matrix((LANES + 2 * HALF, LANES), 0))
    columns[...] = jnp.concatenate([high, low], axis=1)
    for rows in (inner, rim):
        count = rows.shape[0] // 2
        high, low = split(band_matrix((count, count + 2 * HALF), 1))
        rows[...] = jnp.concatenate(
            [jnp.concatenate([high, high], axis=1), jnp.concatenate([low, jnp.zeros_like(low)], axis=1)], axis=0
        )


def split(values):
    high = values.astype(jnp.bfloat16)
    low = (values - high.astype(jnp.float32)).astype(jnp.bfloat16)
    return high, low


def dot(left, right):
    return jnp.dot(left, right, preferred_element_type=jnp.float32)


def column_block(window, band):
    high, low = split(window)
    depth = window.shape[1]
    both = dot(high, band[:depth])
    return both[:, :LANES] + both[:, LANES:] + dot(low, band[:depth, :LANES])


def row_block(window, band):
    high, low = split(window)
    rows = band.shape[0] // 2
    both = dot(band, jnp.concatenate([high, low], axis=0))
    return both[:rows] + both[rows:]


def edge_flags():
    place = lax.axis_index("cols")
    return (place > 0).astype(jnp.float32), (place < lax.axis_size("cols") - 1).astype(jnp.float32)


def row_parity(flip):
    return lax.rem(lax.axis_index("rows") + flip, 2)


def chunks(width, step):
    return [(start, min(start + step, width)) for start in range(0, width, step)]


def edge_sides():
    return [lax.axis_index("cols") == 0] if lax.axis_size("cols") == 2 else [True, False]


def edge_tiles(values, outs):
    width = values.shape[1]
    for out, right in zip(outs, edge_sides()):
        start = pl.multiple_of(jnp.where(right, width - LANES, 0), LANES)
        out[...] = values[:, pl.ds(start, LANES)]


def log_edge_kernel(logs, taps, kept, *outs):
    edge_tiles(logs, outs)
    for out in outs:
        out[...] = jnp.exp(out[...])
    kept[...] = logs[...]


def half_sends(which, flip, across, first, second):
    height, share = across.shape[0], first.shape[1] - LANES
    odd = row_parity(flip)
    lanes = pl.ds(pl.multiple_of(half_place(which) * share, LANES), share + LANES)
    first[...] = across[pl.ds(pl.multiple_of((1 - odd) * (height - HALF), HALF), HALF), lanes]
    second[...] = across[pl.ds(pl.multiple_of(odd * (height - HALF), HALF), HALF), lanes]


def mass_edge_kernel(masses, across, after, first, second, *outs):
    half_sends("own", 1, across, first, second)
    edge_tiles(masses, outs)


def spread_kernel(logs, taps, across, wide):
    width = logs.shape[1]
    edge = 2 * HALF
    wide[:, edge : edge + width] = jnp.exp(logs[...])
    for start in range(LANES, width, LANES):
        across[:, start : start + LANES] = column_block(wide[:, start : start + LANES + 2 * HALF], taps[...])


def spread_edge_kernel(partial, logs, from_left, from_right, taps, across, first, second):
    has_left, has_right = edge_flags()
    height, width = logs.shape
    edge = 2 * HALF
    left = jnp.concatenate([from_left[:, edge:] * has_left, jnp.exp(logs[:, :LANES])], axis=1)
    right = jnp.concatenate([jnp.exp(logs[:, width - edge :]), from_right[:, :edge] * has_right], axis=1)
    across[:, :LANES] = column_block(left, taps[...])
    across[:, width : width + LANES] = column_block(right, taps[...])
    half_sends("other", 0, across, first, second)


def ratio_of(masses, smooth):
    return jnp.where(masses > 0.0, masses / smooth, 0.0)


def column_pass(ratios, taps, out):
    for start in range(0, out.shape[1], LANES):
        out[:, start : start + LANES] = column_block(ratios[:, start : start + LANES + 2 * HALF], taps[...])


def own_weight(weights):
    mine = lax.broadcasted_iota(jnp.int32, weights.shape, 1) == lax.axis_index("hist")
    own = jnp.sum(jnp.where(mine, weights[...], 0.0), axis=1, keepdims=True)
    return own / jnp.sum(weights[...], axis=1, keepdims=True)


def inner_ratio_kernel(
    across, masses, from_left, from_right, weights, taps, row_taps, out, wide, weight, smooth, ratios
):
    weight[...] = jnp.broadcast_to(own_weight(weights), weight.shape)
    has_left, has_right = edge_flags()
    height = masses.shape[0]
    wide[...] = jnp.concatenate(
        [
            from_left[:, LANES - HALF :] * has_left,
            masses[...],
            from_right[:, :HALF] * has_right,
            jnp.zeros((height, 2 * HALF), jnp.float32),
        ],
        axis=1,
    )
    for start, stop in chunks(across.shape[1], 256):
        smooth[:, start:stop] = row_block(across[:, start:stop], row_taps[...])
    ratios[...] = ratio_of(wide[HALF : height - HALF, :], smooth[...])
    column_pass(ratios, taps, out)


def half_place(which):
    place = lax.axis_index("hist") if lax.axis_size("hist") == 2 else 0
    return 1 - place if which == "other" else place


def rim_ratio_kernel(
    which, came, across, first, second, wide, taps, row_taps, after, rims, smooth, ratios
):
    height = across.shape[0]
    share = rims.shape[1]
    odd = row_parity(came)
    offset = half_place(which) * share
    for start, stop in chunks(share + LANES, 256):
        lanes = pl.ds(pl.multiple_of(offset + start, LANES), stop - start)
        one, two = first[:, start:stop], second[:, start:stop]
        upper = jnp.concatenate([jnp.where(odd == 1, one, two), across[: 2 * HALF, lanes]], axis=0)
        lower = jnp.concatenate([across[height - 2 * HALF :, lanes], jnp.where(odd == 1, two, one)], axis=0)
        smooth[:HALF, start:stop] = row_block(upper, row_taps[...])
        smooth[HALF:, start:stop] = row_block(lower, row_taps[...])
    lanes = pl.ds(pl.multiple_of(offset, LANES), share + LANES)
    masses = jnp.concatenate([wide[:HALF, lanes], wide[height - HALF :, lanes]], axis=0)
    ratios[...] = ratio_of(masses, smooth[...])
    column_pass(ratios, taps, rims)


def inner_log_kernel(which, weight, rims, inner, logs, row_taps, smooth, own):
    height = logs.shape[0]
    share = rims.shape[1]
    offset = half_place(which) * share
    for start, stop in chunks(share, 256):
        lanes = pl.ds(pl.multiple_of(offset + start, LANES), stop - start)
        window = jnp.concatenate([rims[:HALF, start:stop], inner[:, lanes], rims[HALF:, start:stop]], axis=0)
        smooth[:, start:stop] = jnp.log(row_block(window, row_taps[...]))
    lanes = pl.ds(pl.multiple_of(offset, LANES), share)
    own[...] = weight[:1, :1] * (logs[HALF : height - HALF, lanes] + smooth[...])


def rim_sends_kernel(goes, rims, after, sent_first, sent_second):
    odd = row_parity(goes)
    sent_first[...] = rims[pl.ds(pl.multiple_of((1 - odd) * HALF, HALF), HALF), :]
    sent_second[...] = rims[pl.ds(pl.multiple_of(odd * HALF, HALF), HALF), :]


def rim_log_kernel(which, came, weight, from_first, from_second, rims, inner, logs, row_taps, after, smooth, own):
    height = logs.shape[0]
    depth = inner.shape[0]
    share = rims.shape[1]
    odd = row_parity(came)
    offset = half_place(which) * share
    for start, stop in chunks(share, 256):
        lanes = pl.ds(pl.multiple_of(offset + start, LANES), stop - start)
        one, two = from_first[:, start:stop], from_second[:, start:stop]
        above, below = jnp.where(odd == 1, one, two), jnp.where(odd == 1, two, one)
        upper = jnp.concatenate([above, rims[:HALF, start:stop], inner[:HALF, lanes]], axis=0)
        lower = jnp.concatenate([inner[depth - HALF :, lanes], rims[HALF:, start:stop], below], axis=0)
        smooth[:HALF, start:stop] = jnp.log(row_block(upper, row_taps[...]))
        smooth[HALF:, start:stop] = jnp.log(row_block(lower, row_taps[...]))
    lanes = pl.ds(pl.multiple_of(offset, LANES), share)
    log_rows = jnp.concatenate([logs[:HALF, lanes], logs[height - HALF :, lanes]], axis=0)
    own[...] = weight[:1, :1] * (log_rows + smooth[...])


def folded(values):
    rows, width = values.shape
    total = jnp.sum(values.reshape(rows // 8, 8, width), axis=0)
    return sum(total[:, start : start + LANES] for start in range(0, width, LANES))


def mean_part(own, smooth, arrived, mean, change):
    log_mean = own[...] + arrived[...]
    values = jnp.exp(log_mean)
    mean[...] = values
    change[...] = log_mean - smooth[...]
    return folded(values)


def inner_mean_kernel(own, smooth, arrived, after, mean, change, partial):
    partial[...] = mean_part(own, smooth, arrived, mean, change)


def later_kernel(rim_own, inner_own, after, later):
    rest = later.shape[0] - HALF
    later[:HALF, :] = rim_own[:HALF, :]
    later[HALF:rest, :] = inner_own[...]
    later[rest:, :] = rim_own[HALF:, :]


def rim_mean_kernel(own, smooth, arrived, before, mean, change, partial):
    partial[...] = before[...] + mean_part(own, smooth, arrived, mean, change)


def final_kernel(
    cells, total, rim_mean, rim_change, inner_mean, inner_change, rim_own, rim_smooth, inner_own, inner_smooth, later,
    barycenter, new_logs, stage, sems,
):
    height, width = barycenter.shape
    share = width // 2
    rest = height - HALF
    scale = cells / jnp.sum(total[...], axis=(0, 1), keepdims=True)
    log_scale = jnp.log(scale)
    rows = ((slice(0, HALF), slice(0, HALF)), (slice(HALF, rest), slice(None)), (slice(rest, height), slice(HALF, 2 * HALF)))
    copies = []

    def send(k, step, which):
        lanes = pl.ds(pl.multiple_of(half_place(which) * share, LANES), share)
        source = stage.at[k, :, slice(step * share, (step + 1) * share)]
        copy = pltpu.make_async_copy(source, (barycenter, new_logs)[k].at[:, lanes], sems.at[k, step])
        copy.start()
        copies.append(copy)

    for (to, part), mean in zip(rows, (rim_mean, inner_mean, rim_mean)):
        stage[0, to, :share] = mean[part, :] * scale
    send(0, 0, "own")
    for (to, part), change in zip(rows, (rim_change, inner_change, rim_change)):
        stage[1, to, :share] = change[part, :] + log_scale
    send(1, 0, "own")
    for (to, part), own, smooth in zip(rows, (rim_own, inner_own, rim_own), (rim_smooth, inner_smooth, rim_smooth)):
        log_mean = own[part, :] + later[to, :]
        stage[0, to, share:] = jnp.exp(log_mean) * scale
        stage[1, to, share:] = log_mean - smooth[part, :] + log_scale
    send(0, 1, "other")
    send(1, 1, "other")
    for copy in copies:
        copy.wait()


def call(kernel, name, args, outs, scratch=(), cost=0, aliases={}, far_out=False, sems=None):
    shaped = lambda shape: shape if isinstance(shape, jax.ShapeDtypeStruct) else jax.ShapeDtypeStruct(shape, jnp.float32)
    near = pl.BlockSpec(memory_space=pltpu.VMEM)
    far = pl.BlockSpec(memory_space=pl.ANY)
    return pl.pallas_call(
        kernel,
        name=name,
        input_output_aliases=aliases,
        out_shape=tuple(shaped(shape) for shape in outs),
        in_specs=[near for _ in args],
        out_specs=tuple(far if far_out else near for _ in outs),
        scratch_shapes=[pltpu.VMEM(shape, jnp.float32) for shape in scratch]
        + ([pltpu.SemaphoreType.DMA(sems)] if sems else []),
        compiler_params=pltpu.CompilerParams(vmem_limit_bytes=32 * 1024 * 1024),
        cost_estimate=pl.CostEstimate(flops=5 * cost, bytes_accessed=cost // 256, transcendentals=0),
    )(*args)


def swap_columns(edges):
    count = lax.axis_size("cols")
    if count == 2:
        got = lax.ppermute(edges[0], "cols", [(0, 1), (1, 0)])
        return got, got
    steps = [(i, i + 1) for i in range(count - 1)]
    right_edge, left_edge = edges
    return (
        lax.ppermute(right_edge, "cols", steps),
        lax.ppermute(left_edge, "cols", [(b, a) for a, b in steps]),
    )


def swap_rows(flip, first, second):
    count = lax.axis_size("rows")
    pairs = lambda start: [
        pair for i in range(start, count - 1, 2) for pair in ((i, i + 1), (i + 1, i))
    ]
    return lax.ppermute(first, "rows", pairs(flip)), lax.ppermute(second, "rows", pairs(1 - flip))


def swap_hist(values):
    return lax.ppermute(values, "hist", [(0, 1), (1, 0)])


def total_over(values, axes):
    count = lax.axis_size(axes)
    if count & (count - 1):
        return lax.psum(values, axes)
    arrived = [lax.ppermute(values, axes, [(i, i ^ mask) for i in range(count)]) for mask in range(1, count)]
    return values + sum(arrived)


def apart(index, mask, span):
    return (index // span ^ mask // span) * span + (index % span ^ mask % span)


def total_aside(values):
    hist, rows, cols = (lax.axis_size(axis) for axis in ("hist", "rows", "cols"))
    if hist & (hist - 1) or cols & (cols - 1):
        return lax.psum(values, ("hist", "cols"))
    aside = cols if rows % 2 == 0 else 0
    total = values
    for k in range(hist):
        for m in range(cols):
            if k or m:
                mask = k * rows * cols + (aside if k else 0) + m
                total = total + lax.ppermute(
                    values, ("hist", "rows", "cols"), [(i, apart(i, mask, rows * cols)) for i in range(hist * rows * cols)]
                )
    return total


def body(hists, log_scaling_fields, histogram_weight_list):
    masses = hists[0]
    logs = log_scaling_fields[0]
    weights = histogram_weight_list
    height, width = masses.shape
    count = lax.axis_size("hist")
    edge = 2 * HALF
    inner = height - edge
    share = width // 2
    wide_width = width + LANES
    matmul = 2 * height * width * 3 * 256
    cells = height * lax.axis_size("rows") * width * lax.axis_size("cols")

    half = lambda *shape: jax.ShapeDtypeStruct(shape, jnp.bfloat16)
    taps, inner_taps, rim_taps = call(
        bands_kernel, "bands", (),
        [half(LANES + edge, 2 * LANES), half(2 * inner, 2 * height), half(edge, 2 * (HALF + edge))],
    )
    flips = {"other": (0, 0), "own": (1, 0)}
    sides = 1 if lax.axis_size("cols") == 2 else 2
    tiles = [(height, LANES)] * sides
    logs, *edges = call(log_edge_kernel, "log_edges", (logs, taps), [(height, width)] + tiles)
    from_left, from_right = swap_columns(edges)
    (partial,) = call(
        spread_kernel, "spread", (logs, taps), [(height, wide_width)], [(height, wide_width)], cost=matmul
    )
    across, *other_sent = call(
        spread_edge_kernel, "spread_edge", (partial, logs, from_left, from_right, taps),
        [(height, wide_width)] + [(HALF, share + LANES)] * 2, cost=matmul // 8, aliases={0: 0},
    )
    first, second, *edges = call(
        mass_edge_kernel, "mass_edges", (masses, across, other_sent[0]), [(HALF, share + LANES)] * 2 + tiles,
        cost=20 * matmul,
    )
    own_sent = (first, second)
    from_left, from_right = swap_columns(edges)
    other_arrived = swap_rows(0, *other_sent)
    own_arrived = swap_rows(1, *own_sent)
    inside, masses, weight = call(
        inner_ratio_kernel, "inner_ratio",
        (across, masses, from_left, from_right, weights.reshape(1, count), taps, inner_taps),
        [(inner, width), (height, wide_width), (8, LANES)], [(inner, wide_width), (inner, wide_width)],
    )

    def rim_ratio(which, arrived, after):
        return call(
            functools.partial(rim_ratio_kernel, which, flips[which][0]), which + "_rim_ratio",
            (across, *arrived, masses, taps, rim_taps, after),
            [(edge, share)], [(edge, share + LANES)] * 2, cost=matmul,
        )[0]

    def inner_log(which, rims):
        return call(
            functools.partial(inner_log_kernel, which), which + "_inner_log",
            (weight, rims, inside, logs, inner_taps), [(inner, share)] * 2, cost=matmul,
        )

    def rim_log(which, rims, arrived, after):
        return call(
            functools.partial(rim_log_kernel, which, flips[which][1]), which + "_rim_log",
            (weight, *arrived, rims, inside, logs, rim_taps, after), [(edge, share)] * 2, cost=matmul,
        )

    def rim_exchange(which, rims, after):
        goes = flips[which][1]
        sent = call(
            functools.partial(rim_sends_kernel, goes), which + "_rim_sends", (rims, after), [(HALF, share)] * 2,
            cost=0 * matmul,
        )
        return swap_rows(goes, *sent)

    other_rims = rim_ratio("other", other_arrived, inside)
    other_inner_smooth, other_inner_own = inner_log("other", other_rims)
    other_arrived = rim_exchange("other", other_rims, other_inner_own)
    own_rims = rim_ratio("own", own_arrived, other_inner_own)
    inner_smooth, inner_own = inner_log("own", own_rims)
    own_arrived = rim_exchange("own", own_rims, inner_own)
    other_rim_smooth, other_rim_own = rim_log("other", other_rims, other_arrived, inner_own)
    rim_smooth, rim_own = rim_log("own", own_rims, own_arrived, other_rim_own)

    if count != 2:
        joined = lambda rim, inside: jnp.concatenate([rim[:HALF], inside, rim[HALF:]], axis=0)
        both = lambda *parts: jnp.concatenate([joined(*parts[:2]), joined(*parts[2:])], axis=1)
        log_mean = lax.psum(both(rim_own, inner_own, other_rim_own, other_inner_own), "hist")
        log_smooth = both(rim_smooth, inner_smooth, other_rim_smooth, other_inner_smooth)
        mean = jnp.exp(log_mean)
        scale = cells / lax.psum(jnp.sum(mean), ("rows", "cols"))
        return (mean * scale, (log_mean + jnp.log(scale) - log_smooth)[None])

    inner_arrived = swap_hist(other_inner_own)
    rim_arrived = swap_hist(other_rim_own)
    inner_mean, inner_change, mass = call(
        inner_mean_kernel, "inner_mean", (inner_own, inner_smooth, inner_arrived, rim_own),
        [(inner, share), (inner, share), (8, LANES)], cost=matmul // 4,
    )
    turn = lax.ppermute(mass, "cols", [(i, i ^ 1) for i in range(lax.axis_size("cols") // 2 * 2)])
    (later,) = call(later_kernel, "later", (rim_own, inner_own, turn), [(height, share)], cost=matmul // 4)
    rim_mean, rim_change, mass = call(
        rim_mean_kernel, "rim_mean", (rim_own, rim_smooth, rim_arrived, mass),
        [(edge, share), (edge, share), (8, LANES)], cost=10 * matmul,
    )
    later_arrived = swap_hist(later)
    mass = total_over(mass, ("rows",))
    mass = total_aside(mass)
    barycenter, new_logs = call(
        functools.partial(final_kernel, float(cells)), "final",
        (mass, rim_mean, rim_change, inner_mean, inner_change, other_rim_own, other_rim_smooth, other_inner_own,
         other_inner_smooth, later_arrived),
        [(height, width)] * 2, [(2, height, width)], far_out=True, sems=(2, 2), cost=matmul // 4,
    )
    return (barycenter, new_logs[None])


def solution(mesh):
    return jax.shard_map(
        body,
        mesh=mesh,
        in_specs=(
            P("hist", ("groups", "rows"), "cols"),
            P("hist", ("groups", "rows"), "cols"),
            P(),
        ),
        out_specs=(P(("groups", "rows"), "cols"), P("hist", ("groups", "rows"), "cols")),
        check_vma=False,
    )
```
